256 devices in a mesh: ctx: 16 (over y, x), exp: 16 (over z, core).
Axes of the slice: x: 4, y: 4, z: 8, core: 2. Of those that a mesh axis runs over, the one named last changes fastest.
Arguments:
- query_raw: bfloat16 [16384, 2048], P('ctx', 'exp'), may hold values from -6 to 6
- key_raw: bfloat16 [16384, 2048], P('ctx', 'exp'), may hold values from -8 to 8
- values: bfloat16 [16384, 4096], P('ctx', 'exp'), may hold values from -6 to 6
- out_gate: bfloat16 [16384, 4096], P('ctx', 'exp'), may hold values from -6 to 6
- log_decay: float32 [32, 16384], P('exp', 'ctx'), may hold values from -0.8 to 0, as said below
- beta_rate: float32 [32, 16384], P('exp', 'ctx'), may hold values from 0 to 1
- head_gain: float32 [128], replicated, may hold values from 0.1 to 1.9
- out_weight: bfloat16 [4096, 2048], P('exp'), may hold values from -0.09375 to 0.09375
- residual: bfloat16 [16384, 2048], P(('ctx', 'exp')), may hold values from -3 to 3
- post_gain: float32 [2048], replicated, may hold values from 0.1 to 1.9
- router_weight: bfloat16 [2048, 256], replicated, may hold values from -0.0625 to 0.0625
- routes: int32 [16384, 10], P(('ctx', 'exp')), may hold values from 0 to 255, all different within a row; in each aligned block of 64 rows (0 to 63, 64 to 127, ...) at most 4 rows name the same one
- placement: int32 [256], replicated, may hold values from 0 to 255, each once
- expert_in: bfloat16 [256, 2048, 1024], P(('ctx', 'exp')), may hold values from -0.125 to 0.125
- expert_out: bfloat16 [256, 512, 2048], P(('ctx', 'exp')), may hold values from -0.5 to 0.5
Outputs:
- core_out: bfloat16 [16384, 4096], P('ctx', 'exp')
- layer_out: bfloat16 [16384, 2048], P(('ctx', 'exp'))
The draws below stay inside these ranges and needn't reach their ends.
Inputs may be any that keep to these rules, and one draw needn't show every extreme that they name: `routes`: each row names 10 different experts; among the 64 rows of one device (aligned blocks of rows) no expert is named by more than 4 rows. A permutation: expert e's weights are entry placement[e] of expert_in and expert_out. `log_decay`: negative.
All inputs are finite; a program needn't handle non-finite values.
Results may differ from the reference program's by a relative error of at most 0.03.
Values may be sent and summed in bfloat16 or wider, within the bound.
No kernel may reach another device: no remote copies, remote signals or barrier semaphores. Data moves between devices by JAX's collectives and lax.ppermute only.
A program may use at most 128 MiB of HBM per device.

```python
import math
import jax
import jax.numpy as jnp
import numpy as np
from jax import lax

D = 2048
HK = 16
HV = 32
K = 128
V = 128
FF = 512
TOP = 10
BLOCK = 64
TOK_CTX = 1024
TOKENS = 16384
TOK_MOE = 64
EXPERTS = 256
CAP = 4
N_EXP = 16


def slow_heads(key, count):
    order = jax.random.permutation(jax.random.fold_in(key, 5), HV)
    return order < count


def draw_key_raw(key, part):
    key = jax.random.fold_in(key, 23)
    keys = jax.random.split(key, 1)
    noise = jax.random.normal(keys[0], (TOKENS, HK * K), jnp.float32)
    mixed = noise
    return jnp.clip(mixed, -8.0, 8.0).astype(jnp.bfloat16)


def draw_log_decay(key, part):
    gradual_decay = slow_heads(key, HV // 2)
    key = jax.random.fold_in(key, 21)
    keys = jax.random.split(key, 6)
    fast_rate = jnp.exp(jax.random.uniform(keys[0], (HV, 1), jnp.float32, math.log(1.0 / 50.0), math.log(1.0 / 30.0)))
    slow_rate = jnp.exp(jax.random.uniform(keys[1], (HV, 1), jnp.float32, math.log(0.2), math.log(0.8))) / TOKENS
    learning_speed = jnp.where(gradual_decay[:, None], slow_rate, fast_rate)
    coarse_estimate = jax.random.uniform(keys[2], (HV, TOKENS), jnp.float32, 0.5, 1.5)
    partition_scale = jnp.exp(jax.random.uniform(keys[3], (HV, TOKENS // TOK_CTX), jnp.float32, math.log(0.6), math.log(1.6)))
    partition_scale = jnp.repeat(partition_scale, TOK_CTX, axis=1)
    spots = jax.random.randint(keys[4], (3,), 0, TOKENS)
    removed_entries = jnp.any(jnp.arange(TOKENS)[None, :] == spots[:, None], axis=0)
    retained_values = jax.random.uniform(keys[5], (HV, TOKENS), jnp.float32, 0.5, 0.8)
    sudden_surge = jnp.where(gradual_decay[:, None] & removed_entries[None, :], jnp.log(retained_values), 0.0)
    return -learning_speed * coarse_estimate * partition_scale + sudden_surge


def draw_beta_rate(key, part):
    gradual_decay = slow_heads(key, HV // 2)
    fast_low = 0.2
    fast_high = 0.9
    key = jax.random.fold_in(key, 22)
    keys = jax.random.split(key, 2)
    slow_beta = jax.random.uniform(keys[0], (HV, TOKENS), jnp.float32, 0.2, 0.8) * (K / TOKENS)
    fast_beta = jax.random.uniform(keys[1], (HV, TOKENS), jnp.float32, fast_low, fast_high)
    return jnp.where(gradual_decay[:, None], slow_beta, fast_beta)


def shard_levels(stream_key, extent, pieces, least, top_value):
    gain, own = 1.0, jax.random.fold_in(stream_key, 6)
    for axis_at, blocks in pieces:
        heights = jnp.exp(jax.random.uniform(jax.random.fold_in(own, axis_at), (blocks,), jnp.float32, least / len(pieces), top_value / len(pieces)))
        gain = gain * jnp.repeat(heights, extent[axis_at] // blocks).reshape([-1 if axis == axis_at else 1 for axis in range(len(extent))])
    return gain


def assign_block(rng, own, number, rows, amount, top, reach, slope):
    order = jax.random.permutation(rng, amount)
    crowded, usual = shares(amount, rows * top, reach, slope, True), shares(amount, rows * top, reach, slope, False)
    places = jnp.arange(amount)

    def named(sizes, rotation):
        used = int((sizes > 0).sum())
        fixed = max(1, used // 4)
        moved = fixed + (places - fixed + rotation * (used - fixed)) % max(1, amount - fixed)
        return jnp.zeros((amount,), jnp.int32).at[order[jnp.where(places < fixed, places, moved)]].set(jnp.asarray(sizes, jnp.int32))

    sizes = jnp.where(number % 4 == 0, named(crowded, number // 4), named(usual, number - number // 4 - 1))
    mixed = jax.random.permutation(jax.random.fold_in(own, 3), amount)
    giver, taker = mixed[0:amount // 2 * 2:2], mixed[1:amount // 2 * 2:2]
    slack = jnp.minimum(sizes[giver] - 1, reach - sizes[taker]) // 2
    slack = jnp.where((giver == order[0]) | (taker == order[0]) | (sizes[taker] == 0), 0, jnp.maximum(slack, 0))
    moved = jax.random.randint(jax.random.fold_in(own, 4), (amount // 2,), 0, 1 << 20) % (slack + 1)
    sizes = sizes.at[giver].add(-moved).at[taker].add(moved)
    members = jnp.searchsorted(jnp.cumsum(sizes), jnp.arange(rows * top), side="right").astype(jnp.int32)
    listing = members.reshape(top, rows).T
    listing = listing[jax.random.permutation(jax.random.fold_in(own, 1), rows)]
    rotation = jax.random.randint(jax.random.fold_in(own, 2), (rows, 1), 0, top)
    return jnp.take_along_axis(listing, (jnp.arange(top)[None, :] + rotation) % top, axis=1)


def shares(count, total, most, lean, full):
    weights = [(1 << 20) // math.isqrt(grade ** lean) + 1 for grade in range(1, count + 1)]
    largest = most if full else min(most, max(-(-total // count), total * weights[0] // sum(weights)))
    least = 1 if total - largest >= count - 1 else 0
    given, surplus = [largest] + [least] * (count - 1), total - largest - least * (count - 1)
    while surplus > 0:
        free = [i for i in range(1, count) if given[i] < largest] or [i for i in range(1, count) if given[i] < most]
        pool, left = sum([weights[i] for i in free]), surplus
        for i in free:
            extra = min(most - given[i], max(1, left * weights[i] // pool), surplus)
            given[i] = given[i] + extra
            surplus = surplus - extra
    return np.array(given)


def scatter_about(own_key, extent, scale, reach, pieces=(), held_as=jnp.bfloat16):
    drawn = scale * jax.random.normal(own_key, extent, jnp.float32)
    if pieces:
        drawn = drawn * shard_levels(own_key, extent, pieces, -0.22, 0.18)
    return jnp.clip(drawn, -reach, reach).astype(held_as)


def setup_inputs(seed: int = 0) -> dict:
    seeds = jax.random.split(jax.random.key(seed), 16)
    query_raw = scatter_about(seeds[0], (TOKENS, HK * K), 1.0, 6.0, ((0, 16), (1, 16)))
    key_raw = draw_key_raw(jax.random.fold_in(seeds[15], 71), 0)
    values = scatter_about(seeds[2], (TOKENS, HV * V), 1.0, 6.0, ((0, 16), (1, 16)))
    out_gate = scatter_about(seeds[3], (TOKENS, HV * V), 1.0, 6.0, ((0, 16), (1, 16)))
    log_decay = draw_log_decay(jax.random.fold_in(seeds[15], 71), 0)
    beta_rate = draw_beta_rate(jax.random.fold_in(seeds[15], 71), 0)
    head_gain = jnp.clip(1.0 + 0.18 * jax.random.normal(seeds[6], (V,), jnp.float32), 0.1, 1.9)
    out_weight = scatter_about(seeds[7], (HV * V, D), (HV * V) ** -0.5, 0.09375, ((0, 16),))
    residual = scatter_about(seeds[8], (TOKENS, D), 0.5, 3.0, ((0, 256),))
    post_gain = jnp.clip(1.0 + 0.18 * jax.random.normal(seeds[9], (D,), jnp.float32), 0.1, 1.9)
    router_weight = scatter_about(seeds[10], (D, EXPERTS), (4 * D) ** -0.5, 0.0625)
    routes_keys = jax.random.split(jax.random.fold_in(seeds[11], 1), TOKENS // TOK_MOE)
    routes_turns = jax.random.permutation(jax.random.fold_in(seeds[11], 3), TOKENS // TOK_MOE)
    routes = jax.vmap(lambda own, number: assign_block(jax.random.fold_in(seeds[11], 2), own, number, TOK_MOE, EXPERTS, TOP, CAP, 2))(routes_keys, routes_turns).reshape((TOKENS, TOP))
    placement = jax.random.permutation(seeds[12], EXPERTS).astype(jnp.int32)
    expert_in = scatter_about(seeds[13], (EXPERTS, D, 2 * FF), D ** -0.5, 0.125, ((0, 256),))
    expert_out = scatter_about(seeds[14], (EXPERTS, FF, D), (FF // 4) ** -0.5, 0.5, ((0, 256),))
    return {"query_raw": query_raw, "key_raw": key_raw, "values": values, "out_gate": out_gate, "log_decay": log_decay, "beta_rate": beta_rate, "head_gain": head_gain, "out_weight": out_weight, "residual": residual, "post_gain": post_gain, "router_weight": router_weight, "routes": routes, "placement": placement, "expert_in": expert_in, "expert_out": expert_out}


EPS = 1e-06
HIGH = lax.Precision.HIGHEST

def unit_rows(matrix):
    return matrix / jnp.sqrt(lax.optimization_barrier(jnp.sum(matrix * matrix, axis=-1, keepdims=True)) + EPS)

def lower_solve(system, rhs):
    return lax.linalg.triangular_solve(system, rhs, left_side=True, lower=True, unit_diagonal=True)

def block_parts(query, keys, vals, decay, learning_speed):
    width = decay.shape[-1]
    index = jnp.arange(width, dtype=jnp.int32)
    strict = index[:, None] > index[None, :]
    within = index[:, None] >= index[None, :]
    cumul = jnp.cumsum(decay, axis=-1)
    spread = cumul[..., :, None] - cumul[..., None, :]
    fall_strict = jnp.where(strict, jnp.exp(jnp.where(strict, spread, 0.0)), 0.0)
    fall_within = jnp.where(within, jnp.exp(jnp.where(within, spread, 0.0)), 0.0)
    inner = jnp.einsum('...ik,...jk->...ij', keys, keys, precision=HIGH)
    system = jnp.eye(width, dtype=jnp.float32) + learning_speed[..., :, None] * fall_strict * inner
    scaled_keys = (learning_speed * jnp.exp(cumul))[..., None] * keys
    wvec = lower_solve(system, scaled_keys)
    uvec = lower_solve(system, learning_speed[..., None] * vals)
    last = cumul[..., -1:]
    qk_mix = jnp.einsum('...ik,...jk->...ij', query, keys, precision=HIGH) * fall_within
    q_decayed = jnp.exp(cumul)[..., None] * query
    k_decayed = jnp.exp(last - cumul)[..., None] * keys
    return (wvec, uvec, qk_mix, q_decayed, k_decayed, last)

def sweep(carry, part):
    wvec, uvec, qk_mix, q_decayed, k_decayed, last = part
    fresh = uvec - jnp.einsum('...ck,...kv->...cv', wvec, carry, precision=HIGH)
    output = jnp.einsum('...ck,...kv->...cv', q_decayed, carry, precision=HIGH)
    output = output + jnp.einsum('...cj,...jv->...cv', qk_mix, fresh, precision=HIGH)
    carry = jnp.exp(last)[..., None] * carry + jnp.einsum('...ck,...cv->...kv', k_decayed, fresh, precision=HIGH)
    return (carry, output)

def reference(query_raw, key_raw, values, out_gate, log_decay, beta_rate, head_gain, out_weight, residual, post_gain, router_weight, routes, placement, expert_in, expert_out):
    ratio = HV // HK
    blocks = TOKENS // BLOCK
    queries = unit_rows(query_raw.astype(jnp.float32).reshape(TOKENS, HK, K)) * (1.0 / math.sqrt(K))
    keys = unit_rows(key_raw.astype(jnp.float32).reshape(TOKENS, HK, K))
    vals = values.astype(jnp.float32).reshape(TOKENS, HV, V)

    def one_head(head):
        group = head // ratio
        parts = block_parts(queries[:, group].reshape(blocks, BLOCK, K), keys[:, group].reshape(blocks, BLOCK, K), vals[:, head].reshape(blocks, BLOCK, V), log_decay[head].reshape(blocks, BLOCK), beta_rate[head].reshape(blocks, BLOCK))
        start = jnp.zeros((K, V), jnp.float32)
        ended, outputs = lax.scan(sweep, start, parts)
        return outputs.reshape(TOKENS, V)
    core = jnp.transpose(lax.map(one_head, jnp.arange(HV, dtype=jnp.int32)), (1, 0, 2))
    gate = out_gate.astype(jnp.float32).reshape(TOKENS, HV, V)
    scaled = core / jnp.sqrt(lax.optimization_barrier(jnp.mean(core * core, axis=-1, keepdims=True)) + EPS)
    core_out = (scaled * head_gain * jax.nn.silu(gate)).astype(jnp.bfloat16).reshape(TOKENS, HV * V)
    group_cols = HV * V // N_EXP

    def add_group(total, group):
        cols = lax.dynamic_slice_in_dim(core_out, group * group_cols, group_cols, 1)
        rows = lax.dynamic_slice_in_dim(out_weight, group * group_cols, group_cols, 0)
        term = lax.optimization_barrier(jnp.dot(cols.astype(jnp.float32), rows.astype(jnp.float32), preferred_element_type=jnp.float32).astype(jnp.bfloat16))
        return (total + term.astype(jnp.float32), None)
    attn, unused = lax.scan(add_group, jnp.zeros((TOKENS, D), jnp.float32), jnp.arange(N_EXP, dtype=jnp.int32))
    mid = lax.optimization_barrier((residual.astype(jnp.float32) + attn).astype(jnp.bfloat16)).astype(jnp.float32)
    normed = (mid / jnp.sqrt(lax.optimization_barrier(jnp.mean(mid * mid, axis=-1, keepdims=True)) + EPS) * post_gain).astype(jnp.bfloat16)
    logits = jnp.dot(normed.astype(jnp.float32), router_weight.astype(jnp.float32), preferred_element_type=jnp.float32)
    picked = jnp.take_along_axis(logits, routes, axis=1)
    raised = jnp.exp(picked)
    gates = raised / lax.optimization_barrier(jnp.sum(raised, axis=1, keepdims=True))
    flat_ids = routes.reshape(-1)
    order = jnp.argsort(flat_ids, stable=True).astype(jnp.int32)
    counts = jnp.bincount(flat_ids, length=EXPERTS).astype(jnp.int32)
    starts = (jnp.cumsum(counts) - counts).astype(jnp.int32)
    most = EXPERTS * CAP
    padded = jnp.concatenate([order, jnp.zeros((most,), jnp.int32)])
    flat_gates = gates.reshape(-1)

    def add_expert(total, expert):
        picks = lax.dynamic_slice_in_dim(padded, starts[expert], most, 0)
        valid = jnp.arange(most, dtype=jnp.int32) < counts[expert]
        token_rows = picks // TOP
        rows = normed[token_rows]
        holder = placement[expert]
        hidden = jnp.dot(rows.astype(jnp.float32), expert_in[holder].astype(jnp.float32), preferred_element_type=jnp.float32)
        act = (jax.nn.silu(hidden[:, :FF]) * hidden[:, FF:]).astype(jnp.bfloat16)
        result = lax.optimization_barrier(jnp.dot(act.astype(jnp.float32), expert_out[holder].astype(jnp.float32), preferred_element_type=jnp.float32).astype(jnp.bfloat16))
        share = jnp.where(valid, flat_gates[picks], 0.0)
        return (total.at[token_rows].add(share[:, None] * result.astype(jnp.float32)), None)
    mixture, unused = lax.scan(add_expert, jnp.zeros((TOKENS, D), jnp.float32), jnp.arange(EXPERTS, dtype=jnp.int32))
    layer_out = (mid + mixture).astype(jnp.bfloat16)
    return (core_out, layer_out)
```

```python
import math

import jax
import jax.numpy as jnp
from jax import lax
from jax.experimental import pallas as pl
from jax.experimental.pallas import tpu as pltpu
from jax.sharding import PartitionSpec as P

F32=jnp.float32; BF=jnp.bfloat16
EPS=1e-6
C=64
K=128
UNROLL = 4

def mm(a,b):
    return lax.dot_general(a,b,(((1,),(0,)),((),())),preferred_element_type=F32)

def split(a):
    hi=a.astype(BF)
    return hi,(a-hi.astype(F32)).astype(BF)

def mm3(a,b):
    ah,al=split(a); bh,bl=split(b)
    return mm(ah,bh)+(mm(al,bh)+mm(ah,bl))

def mm1(a,b):
    return mm(a.astype(BF),b.astype(BF))

def delta_kernel(q_ref,k_ref,v_ref,row_ref,col_ref,go_g,go_o,z_out,wq_s,u_s,p_s,kw_s,dr_s,z_s,el_s):
    n=q_ref.shape[0]//C
    rows=lax.broadcasted_iota(jnp.int32,(2*C,2*C),0)
    cols=lax.broadcasted_iota(jnp.int32,(2*C,2*C),1)
    same=(rows//C)==(cols//C)
    strict=same&(rows>cols)
    within=same&(rows>=cols)
    lane=lax.broadcasted_iota(jnp.int32,(2*C,128),1)
    half=lax.broadcasted_iota(jnp.int32,(2*C,1),0)<C
    levels=[]
    b=1
    while b<C:
        levels.append(strict&((rows//(2*b))==(cols//(2*b)))&((rows//b)!=(cols//b)))
        b*=2
    def unit(m):
        return m*lax.rsqrt(jnp.sum(m*m,axis=-1,keepdims=True)+EPS)
    def prep(step,carry):
        amat=[];xs=[];rhs=[];kts=[];ids=[]
        allc=col_ref[...]
        for u in range(UNROLL):
            c=step*UNROLL+u
            ids.append(c)
            at=pl.ds(pl.multiple_of(c*C,C),C)
            kk=unit(k_ref[at,:].astype(F32))
            qq=unit(q_ref[at,:].astype(F32))*(1.0/math.sqrt(K))
            k2=jnp.concatenate([kk,kk],0)
            q2=jnp.concatenate([qq,qq],0)
            kt=k2.T
            mix=mm3(jnp.concatenate([k2,q2],0),kt)
            g_row=row_ref[pl.ds(c,1),:]
            last_row=row_ref[pl.ds(n+c,1),:]
            g_col=jnp.sum(jnp.where(lane==c,allc,0.0),axis=1,keepdims=True)
            b_col=jnp.sum(jnp.where(lane==n+c,allc,0.0),axis=1,keepdims=True)
            fall=jnp.exp(jnp.where(within,g_col-g_row,0.0))
            a=jnp.where(strict,fall*b_col*mix[:2*C],0.0)
            p_s[c]=jnp.where(within,fall*mix[2*C:],0.0).astype(BF)
            eg=jnp.exp(g_col)
            vv=v_ref[at,:].astype(F32)
            v2=jnp.concatenate([vv[:,:K],vv[:,K:]],0)
            rhs.append(jnp.concatenate([(b_col*eg)*k2,b_col*v2],1))
            wq_s[c,1]=(eg*q2).astype(BF)
            kts.append(kt*jnp.exp(last_row-g_row))
            el_s[c]=jnp.exp(last_row)
            amat.append(a)
            xs.append(jnp.where(rows==cols,1.0,0.0)-jnp.where(levels[0],a,0.0))
        for lev in levels[1:]:
            mids=[mm3(jnp.where(lev,a,0.0),x) for a,x in zip(amat,xs)]
            xs=[x-mm3(x,m) for x,m in zip(xs,mids)]
        wus=[mm3(x,r) for x,r in zip(xs,rhs)]
        for c,wu,kt in zip(ids,wus,kts):
            wq_s[c,0]=wu[:,:K].astype(BF)
            u_s[c]=wu[:,K:]
            both=jnp.concatenate([jnp.where(half,wu,0.0),jnp.where(half,0.0,wu)],1)
            td=mm3(kt,both)
            for h in range(2):
                kw_s[h,c]=td[:,h*2*K:h*2*K+K]
                dr_s[h,c]=td[:,h*2*K+K:(h+1)*2*K]
        return carry
    lax.fori_loop(0,n//UNROLL,prep,0)
    eye=jnp.where(lax.broadcasted_iota(jnp.int32,(K,K),0)==lax.broadcasted_iota(jnp.int32,(K,K),1),1.0,0.0)
    start=jnp.concatenate([eye,jnp.zeros((K,K),F32)],1)
    def chain(c,zs):
        new=[]
        el=el_s[c]
        for h in range(2):
            z=zs[h]
            z_s[c,h]=z.astype(BF)
            e=jnp.sum(jnp.where(lax.broadcasted_iota(jnp.int32,(1,2*C),1)==h*C,el,0.0),axis=1,keepdims=True)
            t=e*z-mm3(kw_s[h,c],z)
            new.append(jnp.concatenate([t[:,:K],t[:,K:]+dr_s[h,c]],1))
        return tuple(new)
    zs=lax.fori_loop(0,n,chain,(start,start))
    for h in range(2):
        z_out[h]=zs[h].astype(BF)
    def emit(step,carry):
        for u in range(UNROLL):
            c=step*UNROLL+u
            fresh=[];outs=[]
            for h in range(2):
                z=z_s[c,h]
                w=wq_s[c,0,h*C:(h+1)*C,:]
                q=wq_s[c,1,h*C:(h+1)*C,:]
                r=mm(jnp.concatenate([w,q],0),z)
                f=-r[:C]
                uu=u_s[c,h*C:(h+1)*C,:]
                fresh.append(jnp.concatenate([f[:,:K],f[:,K:]+uu],1))
                outs.append(r[C:])
            out=jnp.concatenate(outs,0)+mm(p_s[c],jnp.concatenate(fresh,0).astype(BF))
            at=pl.ds(pl.multiple_of(c*C,C),C)
            for h in range(2):
                go_g[h,at,:]=out[h*C:(h+1)*C,:K].astype(BF)
                go_o[h,at,:]=out[h*C:(h+1)*C,K:]
        return carry
    lax.fori_loop(0,n//UNROLL,emit,0)

def delta_local(q,k,v,ld,beta):
    t=q.shape[0]; n=t//C
    g=jnp.cumsum(ld.reshape(2,n,C),axis=-1)
    last=jnp.broadcast_to(g[:,:,-1:],g.shape)
    pack=lambda a: jnp.transpose(a,(1,0,2)).reshape(n,2*C)
    row=jnp.concatenate([pack(g),pack(last)],0)
    col=jnp.zeros((2*C,128),F32)
    col=jnp.concatenate([pack(g).T,pack(beta.reshape(2,n,C)).T,jnp.zeros((2*C,128-2*n),F32)],1)
    vm=pl.BlockSpec(memory_space=pltpu.VMEM)
    return pl.pallas_call(
        delta_kernel,
        out_shape=(jax.ShapeDtypeStruct((2,t,K),BF),jax.ShapeDtypeStruct((2,t,K),F32),jax.ShapeDtypeStruct((2,K,2*K),BF)),
        in_specs=[vm]*5,out_specs=(vm,vm,vm),
        scratch_shapes=[pltpu.VMEM((n,2,2*C,K),BF),pltpu.VMEM((n,2*C,K),F32),pltpu.VMEM((n,2*C,2*C),BF),
            pltpu.VMEM((2,n,K,K),F32),pltpu.VMEM((2,n,K,K),F32),pltpu.VMEM((n,2,K,2*K),BF),pltpu.VMEM((n,1,2*C),F32)],
        compiler_params=pltpu.CompilerParams(vmem_limit_bytes=48*2**20),
    )(q,k,v,row,col)


CAP = 4
GROUP = 4
TOK = 64
SIDE = 4
D = 2048
VM = pl.BlockSpec(memory_space=pltpu.VMEM)


def params(mib):
    return pltpu.CompilerParams(vmem_limit_bytes=mib * 2**20)


def fold_kernel(x_ref, own, a1, a2, a3, total_ref, prefix_ref):
    x = x_ref[0]
    eye = jnp.where(
        lax.broadcasted_iota(jnp.int32, (K, K), 0) == lax.broadcasted_iota(jnp.int32, (K, K), 1),
        1.0,
        0.0,
    )
    for h in range(2):
        near = [own[h].astype(F32), a1[h].astype(F32), a2[h].astype(F32), a3[h].astype(F32)]
        z = jnp.concatenate([eye, jnp.zeros((K, K), F32)], 1)
        prefix = z
        for j in range(SIDE):
            item = near[0]
            for d in range(1, SIDE):
                item = jnp.where((x - j) % SIDE == d, near[d], item)
            if j == 0:
                z = item
            else:
                zh, zl = split(z)
                m = item[:, :K].astype(BF)
                t = mm(m, zh) + mm(m, zl)
                z = jnp.concatenate([t[:, :K], t[:, K:] + item[:, K:]], 1)
            if j < SIDE - 1:
                prefix = jnp.where(x == j + 1, z, prefix)
        total_ref[h] = z.astype(BF)
        prefix_ref[h] = prefix


def core_kernel(par_ref, g_ref, o_ref, prefix, b1, b2, b3, gate_ref, gain_ref, core_ref, mine, sib):
    gain = gain_ref[...]
    even = par_ref[0] == 0
    state = []
    for h in range(2):
        e = b3[h][:, K:].astype(F32)
        for b in (b2, b1):
            eh, el = split(e)
            m = b[h][:, :K]
            e = mm(m, eh) + mm(m, el) + b[h][:, K:].astype(F32)
        e = mm3(prefix[h][:, :K], e) + prefix[h][:, K:]
        eh, el = split(e)
        state.append(jnp.concatenate([eh, el], 1))
    step = 2 * TOK

    def body(i, carry):
        at = pl.ds(pl.multiple_of(i * step, step), step)
        outs = []
        for h in range(2):
            both = mm(g_ref[h, at, :], state[h])
            core = o_ref[h, at, :] + both[:, :K] + both[:, K:]
            gate = gate_ref[at, h * K : (h + 1) * K].astype(F32)
            scaled = core * lax.rsqrt(jnp.mean(core * core, axis=-1, keepdims=True) + EPS)
            outs.append((scaled * gain * (gate / (1.0 + jnp.exp(-gate)))).astype(BF))
        out = jnp.concatenate(outs, 1)
        core_ref[at, :] = out
        to = pl.ds(pl.multiple_of(i * TOK, TOK), TOK)
        mine[to, :] = jnp.where(even, out[:TOK], out[TOK:])
        sib[to, :] = jnp.where(even, out[TOK:], out[:TOK])
        return carry

    lax.fori_loop(0, g_ref.shape[1] // step, body, 0)


def project_kernel(a_ref, b_ref, wa_ref, wb_ref, out_ref):
    out_ref[...] = (mm(a_ref[...], wa_ref[...]) + mm(b_ref[...], wb_ref[...])).astype(BF)


def project(a, b, wa, wb):
    rows, depth = a.shape
    wide = 512
    return pl.pallas_call(
        project_kernel,
        grid=(D // wide,),
        out_shape=jax.ShapeDtypeStruct((rows, D), BF),
        in_specs=[
            pl.BlockSpec((rows, depth), lambda i: (0, 0)),
            pl.BlockSpec((rows, depth), lambda i: (0, 0)),
            pl.BlockSpec((depth, wide), lambda i: (0, i)),
            pl.BlockSpec((depth, wide), lambda i: (0, i)),
        ],
        out_specs=pl.BlockSpec((rows, wide), lambda i: (0, i)),
        compiler_params=params(40),
    )(a, b, wa, wb)


def dispatch_kernel(sel_ref, rows_ref, out_ref):
    out = lax.dot_general(
        sel_ref[...], rows_ref[...], (((0,), (0,)), ((), ())), preferred_element_type=F32
    ).astype(BF)
    out_ref[...] = out.reshape(out_ref.shape)


def dispatch(sel, rows):
    n_ctx = 16
    part = GROUP * TOK
    return pl.pallas_call(
        dispatch_kernel,
        grid=(rows.shape[0] // part,),
        out_shape=jax.ShapeDtypeStruct((n_ctx, TOK, D), BF),
        in_specs=[
            pl.BlockSpec((part, sel.shape[1]), lambda g: (g, 0)),
            pl.BlockSpec((part, D), lambda g: (g, 0)),
        ],
        out_specs=pl.BlockSpec((n_ctx, GROUP * CAP, D), lambda g: (0, g, 0)),
        compiler_params=params(40),
    )(sel, rows)


def expert_kernel(x_ref, up_ref, down_ref, out_ref):
    hidden = mm(x_ref[...], up_ref[...])
    width = down_ref.shape[0]
    gate = hidden[:, :width]
    act = (gate / (1.0 + jnp.exp(-gate)) * hidden[:, width:]).astype(BF)
    out_ref[...] = mm(act, down_ref[...]).astype(BF)


def expert(x, gate_up, down):
    part = 256
    return pl.pallas_call(
        expert_kernel,
        grid=(x.shape[0] // part,),
        out_shape=jax.ShapeDtypeStruct(x.shape, BF),
        in_specs=[
            pl.BlockSpec((part, D), lambda i: (i, 0)),
            pl.BlockSpec(gate_up.shape, lambda i: (0, 0)),
            pl.BlockSpec(down.shape, lambda i: (0, 0)),
        ],
        out_specs=pl.BlockSpec((part, D), lambda i: (i, 0)),
        compiler_params=params(48),
    )(x, gate_up, down)


def combine_kernel(par_ref, w_ref, y_ref, mine, sib):
    even = par_ref[0] == 0
    rows = y_ref[...].reshape(w_ref.shape[1], D)
    out = mm(w_ref[...], rows).astype(BF)
    for i in range(GROUP // 2):
        a = out[2 * i * TOK : (2 * i + 1) * TOK]
        b = out[(2 * i + 1) * TOK : (2 * i + 2) * TOK]
        mine[i * TOK : (i + 1) * TOK, :] = jnp.where(even, a, b)
        sib[i * TOK : (i + 1) * TOK, :] = jnp.where(even, b, a)


def combine(parity, weights, y):
    part = GROUP * TOK
    rows = weights.shape[0]
    half = jax.ShapeDtypeStruct((rows // 2, D), BF)
    return pl.pallas_call(
        combine_kernel,
        grid=(rows // part,),
        out_shape=(half, half),
        in_specs=[
            pl.BlockSpec(memory_space=pltpu.SMEM),
            pl.BlockSpec((part, weights.shape[1]), lambda g: (g, 0)),
            pl.BlockSpec((y.shape[0], GROUP * CAP, D), lambda g: (0, g, 0)),
        ],
        out_specs=(
            pl.BlockSpec((part // 2, D), lambda g: (g, 0)),
            pl.BlockSpec((part // 2, D), lambda g: (g, 0)),
        ),
        compiler_params=params(40),
    )(parity, weights, y)


def along_x(d):
    return [(i, (i // SIDE) * SIDE + (i % SIDE + d) % SIDE) for i in range(SIDE * SIDE)]


def along_y(d):
    return [(i, i + SIDE * d) for i in range(SIDE * (SIDE - d))]


def local(
    query_raw,
    key_raw,
    values,
    out_gate,
    log_decay,
    beta_rate,
    head_gain,
    out_weight,
    residual,
    post_gain,
    router_weight,
    routes,
    placement,
    expert_in,
    expert_out,
):
    n_exp = lax.axis_size("exp")
    experts = router_weight.shape[1]
    at_exp = lax.axis_index("exp")
    at_x = (lax.axis_index("ctx") % SIDE).reshape(1)
    parity = (at_exp % 2).reshape(1)
    core_pairs = [(i, i ^ 1) for i in range(n_exp)]
    same_core = [list(range(0, n_exp, 2)), list(range(1, n_exp, 2))]

    routes_all = lax.all_gather(routes, "exp", tiled=True)
    weight_sib = lax.ppermute(out_weight, "exp", core_pairs)

    g, o, z = delta_local(query_raw, key_raw, values, log_decay, beta_rate)
    near = [lax.ppermute(z, "ctx", along_x(d)) for d in range(1, SIDE)]
    whole = jax.ShapeDtypeStruct(z.shape, BF)
    total, prefix = pl.pallas_call(
        fold_kernel,
        out_shape=(whole, jax.ShapeDtypeStruct(z.shape, F32)),
        in_specs=[pl.BlockSpec(memory_space=pltpu.SMEM)] + [VM] * 4,
        out_specs=(VM, VM),
        compiler_params=params(32),
    )(at_x, z, *near)
    far = [lax.ppermute(total, "ctx", along_y(d)) for d in range(1, SIDE)]
    half = jax.ShapeDtypeStruct((values.shape[0] // 2, values.shape[1]), BF)
    core_out, mine, sib = pl.pallas_call(
        core_kernel,
        out_shape=(jax.ShapeDtypeStruct(values.shape, BF), half, half),
        in_specs=[pl.BlockSpec(memory_space=pltpu.SMEM)] + [VM] * 8,
        out_specs=(VM, VM, VM),
        compiler_params=params(40),
    )(parity, g, o, prefix, *far, out_gate, head_gain.reshape(1, K))

    got = lax.ppermute(sib, "exp", core_pairs)
    terms = project(mine, got, out_weight, weight_sib)
    attn = lax.psum_scatter(
        terms, "exp", scatter_dimension=0, tiled=True, axis_index_groups=same_core
    ).astype(F32)
    mid = lax.optimization_barrier((residual.astype(F32) + attn).astype(BF)).astype(F32)
    normed = (mid / jnp.sqrt(jnp.mean(mid * mid, axis=-1, keepdims=True) + EPS) * post_gain).astype(
        BF
    )
    normed_all = lax.all_gather(normed, "exp", tiled=True)

    rows = routes_all.shape[0]
    ids = jnp.arange(experts, dtype=jnp.int32)
    chosen = jnp.any(routes_all[:, :, None] == ids[None, None, :], axis=1)
    wide = n_exp * GROUP * CAP
    lanes = jnp.arange(wide, dtype=jnp.int32)
    holder = (lanes // (GROUP * CAP)) * n_exp + at_exp
    spread = (placement[:, None] == holder[None, :]).astype(BF)
    named = jnp.dot(chosen.astype(BF), spread, preferred_element_type=F32)
    order = jnp.arange(TOK, dtype=jnp.int32)
    before = (order[:, None] > order[None, :]).astype(BF)
    rank = jnp.einsum(
        "ts,bsl->btl",
        before,
        named.astype(BF).reshape(rows // TOK, TOK, wide),
        preferred_element_type=F32,
    ).reshape(rows, wide)
    block = (jnp.arange(rows, dtype=jnp.int32) // TOK) % GROUP
    sel = (
        (named > 0.5)
        & (rank == (lanes % CAP).astype(F32)[None, :])
        & (block[:, None] == ((lanes // CAP) % GROUP)[None, :])
    )

    logits = jnp.dot(normed_all, router_weight, preferred_element_type=F32)
    raised = jnp.where(chosen, jnp.exp(logits), 0.0)
    gates = raised / jnp.sum(raised, axis=-1, keepdims=True)
    mine_gates = jnp.dot(gates, spread.astype(F32), precision=lax.Precision.HIGHEST)
    weights = jnp.where(sel, mine_gates, 0.0).astype(BF)

    outgoing = dispatch(sel.astype(BF), normed_all)
    arrived = lax.all_to_all(outgoing, "ctx", split_axis=0, concat_axis=0, tiled=True)
    computed = expert(arrived.reshape(-1, D), expert_in[0], expert_out[0]).reshape(arrived.shape)
    returned = lax.all_to_all(computed, "ctx", split_axis=0, concat_axis=0, tiled=True)
    mine_sum, sib_sum = combine(parity, weights, returned)
    got_sum = lax.ppermute(sib_sum, "exp", core_pairs)
    pair = (mine_sum.astype(F32) + got_sum.astype(F32)).astype(BF)
    mixture = lax.psum_scatter(
        pair, "exp", scatter_dimension=0, tiled=True, axis_index_groups=same_core
    ).astype(F32)
    return (core_out, (mid + mixture).astype(BF))


def solution(mesh):
    placed = (
        P("ctx", "exp"),
        P("ctx", "exp"),
        P("ctx", "exp"),
        P("ctx", "exp"),
        P("exp", "ctx"),
        P("exp", "ctx"),
        P(),
        P("exp", None),
        P(("ctx", "exp"), None),
        P(),
        P(),
        P(("ctx", "exp"), None),
        P(),
        P(("ctx", "exp"), None, None),
        P(("ctx", "exp"), None, None),
    )
    return jax.shard_map(
        local,
        mesh=mesh,
        in_specs=placed,
        out_specs=(P("ctx", "exp"), P(("ctx", "exp"), None)),
        check_vma=False,
    )
```

```python
import math

import jax
import jax.numpy as jnp
from jax import lax
from jax.experimental import pallas as pl
from jax.experimental.pallas import tpu as pltpu
from jax.sharding import PartitionSpec as P

F32=jnp.float32; BF=jnp.bfloat16
EPS=1e-6
C=64
K=128
UNROLL = 8

def mm(a,b):
    return lax.dot_general(a,b,(((1,),(0,)),((),())),preferred_element_type=F32)

def split(a):
    hi=a.astype(BF)
    return hi,(a-hi.astype(F32)).astype(BF)

def mm3(a,b):
    ah,al=split(a); bh,bl=split(b)
    n=b.shape[1]
    if n==K:
        r=mm(jnp.concatenate([ah,al],1),jnp.concatenate([jnp.concatenate([bh,bl],1)]*2,0))
        return r[:,:n]+r[:,n:]
    return mm(jnp.concatenate([ah,al],1),jnp.concatenate([bh,bh],0))+mm(ah,bl)

def mm2(a,b):
    bh,bl=split(b)
    return mm(jnp.concatenate([a,a],1),jnp.concatenate([bh,bl],0))

def mm2l(a,b):
    ah,al=split(a)
    return mm(jnp.concatenate([ah,al],1),jnp.concatenate([b,b],0))

def mm1(a,b):
    return mm(a.astype(BF),b.astype(BF))

def delta_kernel(q_ref,k_ref,v_ref,row_ref,col_ref,go_g,go_o,z_out,wq_s,u_s,p_s,kw_s,dr_s,z_s,el_s):
    n=q_ref.shape[0]//C
    rows=lax.broadcasted_iota(jnp.int32,(2*C,2*C),0)
    cols=lax.broadcasted_iota(jnp.int32,(2*C,2*C),1)
    same=(rows//C)==(cols//C)
    strict=same&(rows>cols)
    within=same&(rows>=cols)
    lane=lax.broadcasted_iota(jnp.int32,(2*C,128),1)
    half=lax.broadcasted_iota(jnp.int32,(2*C,1),0)<C
    levels=[]
    b=1
    while b<C:
        levels.append(strict&((rows//(2*b))==(cols//(2*b)))&((rows//b)!=(cols//b)))
        b*=2
    def unit(m):
        return m*lax.rsqrt(jnp.sum(m*m,axis=-1,keepdims=True)+EPS)
    def prep(step,carry):
        amat=[];xs=[];rhs=[];kts=[];ids=[]
        allc=col_ref[...]
        for u in range(UNROLL):
            c=step*UNROLL+u
            ids.append(c)
            at=pl.ds(pl.multiple_of(c*C,C),C)
            kb=k_ref[at,:]
            qb=q_ref[at,:]
            k2=jnp.concatenate([kb,kb],0)
            q2=jnp.concatenate([qb,qb],0)
            kt=k2.T
            raw=mm(jnp.concatenate([k2,q2],0),kt)
            kf=k2.astype(F32)
            qf=q2.astype(F32)
            sk=lax.rsqrt(jnp.sum(kf*kf,axis=-1,keepdims=True)+EPS)
            sq=lax.rsqrt(jnp.sum(qf*qf,axis=-1,keepdims=True)+EPS)*(1.0/math.sqrt(K))
            sk_row=lax.rsqrt(jnp.sum(jnp.where(rows==cols,raw[:2*C],0.0),axis=0,keepdims=True)+EPS)
            g_row=row_ref[pl.ds(c,1),:]
            last_row=row_ref[pl.ds(n+c,1),:]
            b_row=row_ref[pl.ds(2*n+c,1),:]
            g_col=jnp.sum(jnp.where(lane==c,allc,0.0),axis=1,keepdims=True)
            b_col=jnp.sum(jnp.where(lane==n+c,allc,0.0),axis=1,keepdims=True)
            l_col=jnp.sum(jnp.where(lane==2*n+c,allc,0.0),axis=1,keepdims=True)
            fall=jnp.exp(jnp.where(within,g_col-g_row,0.0))*sk_row
            a=jnp.where(strict,fall*(b_col*sk)*raw[:2*C],0.0)
            p_s[c]=jnp.where(within,fall*sq*raw[2*C:],0.0).astype(BF)
            eg=jnp.exp(g_col)
            vb=v_ref[at,:]
            v2=jnp.concatenate([vb[:,:K],vb[:,K:]],0)
            rhs.append((b_row*jnp.exp(g_row)*sk_row,b_row,k2,v2))
            wq_s[c,1]=((eg*sq)*qf).astype(BF)
            kts.append((kt,sk*jnp.exp(l_col-g_col)))
            el_s[c]=jnp.exp(last_row)
            amat.append(a)
            xs.append(jnp.where(rows==cols,1.0,0.0)-jnp.where(levels[0],a,0.0))
        for lev in levels[1:]:
            mids=[mm3(jnp.where(lev,a,0.0),x) for a,x in zip(amat,xs)]
            xs=[x-mm3(x,m) for x,m in zip(xs,mids)]
        for c,x,(wr,br,k2,v2),(kt,kc) in zip(ids,xs,rhs,kts):
            w=mm2l(x*wr,k2)
            u=mm2l(x*br,v2)
            wq_s[c,0]=w.astype(BF)
            u_s[c]=u
            wu=jnp.concatenate([w,u],1)*kc
            both=jnp.concatenate([jnp.where(half,wu,0.0),jnp.where(half,0.0,wu)],1)
            td=mm2(kt,both)
            for h in range(2):
                kw_s[h,c]=td[:,h*2*K:h*2*K+K]
                dr_s[h,c]=td[:,h*2*K+K:(h+1)*2*K]
        return carry
    lax.fori_loop(0,n//UNROLL,prep,0)
    eye=jnp.where(lax.broadcasted_iota(jnp.int32,(K,K),0)==lax.broadcasted_iota(jnp.int32,(K,K),1),1.0,0.0)
    start=jnp.concatenate([eye,jnp.zeros((K,K),F32)],1)
    def chain(c,zs):
        new=[]
        el=el_s[c]
        for h in range(2):
            z=zs[h]
            z_s[c,h]=z.astype(BF)
            e=jnp.sum(jnp.where(lax.broadcasted_iota(jnp.int32,(1,2*C),1)==h*C,el,0.0),axis=1,keepdims=True)
            t=e*z-mm3(kw_s[h,c],z)
            new.append(jnp.concatenate([t[:,:K],t[:,K:]+dr_s[h,c]],1))
        return tuple(new)
    zs=lax.fori_loop(0,n,chain,(start,start),unroll=4)
    for h in range(2):
        z_out[h]=zs[h].astype(BF)
    def emit(step,carry):
        for u in range(UNROLL):
            c=step*UNROLL+u
            fresh=[];outs=[]
            for h in range(2):
                z=z_s[c,h]
                w=wq_s[c,0,h*C:(h+1)*C,:]
                q=wq_s[c,1,h*C:(h+1)*C,:]
                r=mm(jnp.concatenate([w,q],0),z)
                f=-r[:C]
                uu=u_s[c,h*C:(h+1)*C,:]
                fresh.append(jnp.concatenate([f[:,:K],f[:,K:]+uu],1))
                outs.append(r[C:])
            out=jnp.concatenate(outs,0)+mm(p_s[c],jnp.concatenate(fresh,0).astype(BF))
            at=pl.ds(pl.multiple_of(c*C,C),C)
            for h in range(2):
                go_g[h,at,:]=out[h*C:(h+1)*C,:K].astype(BF)
                go_o[h,at,:]=out[h*C:(h+1)*C,K:]
        return carry
    lax.fori_loop(0,n//UNROLL,emit,0)

def whole(shape):
    return pl.BlockSpec(tuple(shape),lambda *_: (0,)*len(shape))

def delta_local(q,k,v,ld,beta):
    t=q.shape[0]; n=t//C
    g=jnp.cumsum(ld.reshape(2,n,C),axis=-1)
    last=jnp.broadcast_to(g[:,:,-1:],g.shape)
    pack=lambda a: jnp.transpose(a,(1,0,2)).reshape(n,2*C)
    rate=pack(beta.reshape(2,n,C))
    row=jnp.concatenate([pack(g),pack(last),rate],0)
    col=jnp.concatenate([pack(g).T,rate.T,pack(last).T,jnp.zeros((2*C,128-3*n),F32)],1)
    shapes=[((2,t,K),BF),((2,t,K),F32),((2,K,2*K),BF)]
    return pl.pallas_call(
        delta_kernel,
        grid=(1,),
        out_shape=[jax.ShapeDtypeStruct(a,d) for a,d in shapes],
        in_specs=[whole(a.shape) for a in (q,k,v,row,col)],out_specs=[whole(a) for a,d in shapes],
        scratch_shapes=[pltpu.VMEM((n,2,2*C,K),BF),pltpu.VMEM((n,2*C,K),F32),pltpu.VMEM((n,2*C,2*C),BF),
            pltpu.VMEM((2,n,K,K),F32),pltpu.VMEM((2,n,K,K),F32),pltpu.VMEM((n,2,K,2*K),BF),pltpu.VMEM((n,1,2*C),F32)],
        compiler_params=pltpu.CompilerParams(vmem_limit_bytes=56*2**20),
    )(q,k,v,row,col)

CAP = 4
GROUP = 4
TOK = 64
SIDE = 4
D = 2048


def params(mib):
    return pltpu.CompilerParams(vmem_limit_bytes=mib * 2**20)


def fold_kernel(x_ref, own, a1, a2, a3, total_ref, prefix_ref):
    x = x_ref[0]
    eye = jnp.where(
        lax.broadcasted_iota(jnp.int32, (K, K), 0) == lax.broadcasted_iota(jnp.int32, (K, K), 1),
        1.0,
        0.0,
    )
    for h in range(2):
        near = [own[h].astype(F32), a1[h].astype(F32), a2[h].astype(F32), a3[h].astype(F32)]
        z = jnp.concatenate([eye, jnp.zeros((K, K), F32)], 1)
        prefix = z
        for j in range(SIDE):
            item = near[0]
            for d in range(1, SIDE):
                item = jnp.where((x - j) % SIDE == d, near[d], item)
            if j == 0:
                z = item
            else:
                zh, zl = split(z)
                m = item[:, :K].astype(BF)
                t = mm(m, zh) + mm(m, zl)
                z = jnp.concatenate([t[:, :K], t[:, K:] + item[:, K:]], 1)
            if j < SIDE - 1:
                prefix = jnp.where(x == j + 1, z, prefix)
        total_ref[h] = z.astype(BF)
        prefix_ref[h] = prefix


def core_kernel(
    par_ref, g_ref, o_ref, prefix, b1, b2, b3, gate_ref, gain_ref, core_ref, mine, sib, state
):
    gain = gain_ref[...]
    even = par_ref[0] == 0

    @pl.when(pl.program_id(0) == 0)
    def _():
        for h in range(2):
            e = b3[h][:, K:].astype(F32)
            for b in (b2, b1):
                eh, el = split(e)
                m = b[h][:, :K]
                e = mm(m, eh) + mm(m, el) + b[h][:, K:].astype(F32)
            e = mm3(prefix[h][:, :K], e) + prefix[h][:, K:]
            eh, el = split(e)
            state[h] = jnp.concatenate([eh, el], 1)

    step = 2 * TOK
    for i in range(g_ref.shape[1] // step):
        at = slice(i * step, (i + 1) * step)
        outs = []
        for h in range(2):
            both = mm(g_ref[h, at, :], state[h])
            core = o_ref[h, at, :] + both[:, :K] + both[:, K:]
            gate = gate_ref[at, h * K : (h + 1) * K].astype(F32)
            scaled = core * lax.rsqrt(jnp.mean(core * core, axis=-1, keepdims=True) + EPS)
            outs.append((scaled * gain * (gate / (1.0 + jnp.exp(-gate)))).astype(BF))
        out = jnp.concatenate(outs, 1)
        core_ref[at, :] = out
        to = slice(i * TOK, (i + 1) * TOK)
        mine[to, :] = jnp.where(even, out[:TOK], out[TOK:])
        sib[to, :] = jnp.where(even, out[TOK:], out[:TOK])


def core_local(parity, g, o, prefix, far, gate, gain):
    rows, wide = gate.shape
    part = 512
    half = jax.ShapeDtypeStruct((rows // 2, wide), BF)
    heads = pl.BlockSpec((2, part, K), lambda i: (0, i, 0))
    half_spec = pl.BlockSpec((part // 2, wide), lambda i: (i, 0))
    full_spec = pl.BlockSpec((part, wide), lambda i: (i, 0))
    return pl.pallas_call(
        core_kernel,
        grid=(rows // part,),
        out_shape=(jax.ShapeDtypeStruct(gate.shape, BF), half, half),
        in_specs=[pl.BlockSpec(memory_space=pltpu.SMEM), heads, heads]
        + [whole(prefix.shape)] * 4
        + [full_spec, whole(gain.shape)],
        out_specs=(full_spec, half_spec, half_spec),
        scratch_shapes=[pltpu.VMEM((2, K, 2 * K), BF)],
        compiler_params=params(56),
    )(parity, g, o, prefix, *far, gate, gain)


def project_kernel(a_ref, b_ref, wa_ref, wb_ref, out_ref):
    out_ref[...] = (mm(a_ref[...], wa_ref[...]) + mm(b_ref[...], wb_ref[...])).astype(BF)


def project(a, b, wa, wb):
    rows, depth = a.shape
    wide = 512
    return pl.pallas_call(
        project_kernel,
        grid=(D // wide,),
        out_shape=jax.ShapeDtypeStruct((rows, D), BF),
        in_specs=[
            pl.BlockSpec((rows, depth), lambda i: (0, 0)),
            pl.BlockSpec((rows, depth), lambda i: (0, 0)),
            pl.BlockSpec((depth, wide), lambda i: (0, i)),
            pl.BlockSpec((depth, wide), lambda i: (0, i)),
        ],
        out_specs=pl.BlockSpec((rows, wide), lambda i: (0, i)),
        compiler_params=params(16),
    )(a, b, wa, wb)


def pick(sel, rows):
    out = lax.dot_general(sel, rows, (((0,), (0,)), ((), ())), preferred_element_type=F32)
    return out.astype(BF).reshape(sel.shape[1] // (GROUP * CAP), GROUP * CAP, D)


def near_kernel(sel_ref, mine_ref, sib_ref, out_ref):
    out_ref[:, : GROUP * CAP, :] = pick(sel_ref[: GROUP * TOK], mine_ref[...])
    out_ref[:, GROUP * CAP :, :] = pick(sel_ref[GROUP * TOK :], sib_ref[...])


def dispatch_near(sel, mine, sib):
    return pl.pallas_call(
        near_kernel,
        grid=(1,),
        out_shape=jax.ShapeDtypeStruct((16, 2 * GROUP * CAP, D), BF),
        in_specs=[whole(sel.shape), whole(mine.shape), whole(sib.shape)],
        out_specs=whole((16, 2 * GROUP * CAP, D)),
        compiler_params=params(16),
    )(sel, mine, sib)


def far_kernel(order_ref, sel_ref, r0, r1, r2, r3, out_ref):
    rows = jnp.concatenate([r0[...], r1[...], r2[...], r3[...]], 0)
    out_ref[...] = pick(sel_ref[...], rows)


def dispatch_far(order, sel, rows):
    part = GROUP * TOK

    def block(j):
        return pl.BlockSpec((TOK, D), lambda g, order: (order[GROUP * g + j], 0))

    return pl.pallas_call(
        far_kernel,
        grid_spec=pltpu.PrefetchScalarGridSpec(
            num_scalar_prefetch=1,
            grid=(2,),
            in_specs=[pl.BlockSpec((part, sel.shape[1]), lambda g, order: (g, 0))]
            + [block(j) for j in range(GROUP)],
            out_specs=pl.BlockSpec((16, GROUP * CAP, D), lambda g, order: (0, g, 0)),
        ),
        out_shape=jax.ShapeDtypeStruct((16, 2 * GROUP * CAP, D), BF),
        compiler_params=params(16),
    )(order, sel, rows, rows, rows, rows)


def expert_kernel(x_ref, gate_ref, up_ref, down_ref, out_ref, total):
    x = x_ref[...]
    gate = mm(x, gate_ref[...])
    act = (gate / (1.0 + jnp.exp(-gate)) * mm(x, up_ref[...])).astype(BF)
    term = mm(act, down_ref[...])
    step = pl.program_id(0)

    @pl.when(step == 0)
    def _():
        total[...] = term

    @pl.when(step > 0)
    def _():
        out_ref[...] = (total[...] + term).astype(BF)


def expert(x, gate_up, down):
    part = down.shape[0] // 2
    return pl.pallas_call(
        expert_kernel,
        grid=(2,),
        out_shape=jax.ShapeDtypeStruct(x.shape, BF),
        in_specs=[
            whole(x.shape),
            pl.BlockSpec((D, part), lambda i: (0, i)),
            pl.BlockSpec((D, part), lambda i: (0, 2 + i)),
            pl.BlockSpec((part, D), lambda i: (i, 0)),
        ],
        out_specs=whole(x.shape),
        scratch_shapes=[pltpu.VMEM(x.shape, F32)],
        cost_estimate=pl.CostEstimate(
            flops=6 * x.shape[0] * D * down.shape[0], bytes_accessed=10 * 2**20, transcendentals=0
        ),
        compiler_params=params(32),
    )(x, gate_up, gate_up, down)


def combine_kernel(w_ref, y_ref, out_ref):
    rows = y_ref[...].reshape(w_ref.shape[1], D)
    out_ref[...] = mm(w_ref[...], rows).astype(BF)


def combine(weights, y, at, half):
    part = GROUP * TOK
    return pl.pallas_call(
        combine_kernel,
        grid=(1,),
        out_shape=jax.ShapeDtypeStruct((part, D), BF),
        in_specs=[
            pl.BlockSpec((part, weights.shape[1]), lambda i: (at, 0)),
            pl.BlockSpec((y.shape[0], GROUP * CAP, D), lambda i: (0, half, 0)),
        ],
        out_specs=pl.BlockSpec((part, D), lambda i: (0, 0)),
        compiler_params=params(16),
    )(weights, y)


def place_kernel(at_ref, own_ref, got_ref, out_ref):
    i = pl.program_id(0)
    total = own_ref[...].astype(F32) + got_ref[...].astype(F32)
    out_ref[...] = jnp.where(at_ref[i] < GROUP, total, 0.0).astype(BF)


def place(at, own, got):
    part = pl.BlockSpec((TOK, D), lambda i, at: (jnp.minimum(at[i], GROUP - 1), 0))
    chips = at.shape[0]
    return pl.pallas_call(
        place_kernel,
        grid_spec=pltpu.PrefetchScalarGridSpec(
            num_scalar_prefetch=1,
            grid=(chips,),
            in_specs=[part, part],
            out_specs=pl.BlockSpec((TOK, D), lambda i, at: (i, 0)),
        ),
        out_shape=jax.ShapeDtypeStruct((chips * TOK, D), BF),
        compiler_params=params(8),
    )(at, own, got)


NEAR = ((0, 1, -1, 2), (0, 1, -1, -2))
FAR = ((-2, 3, -3, 4), (2, 3, -3, 4))


def along_z(i, way, n):
    return [(j, (j + 2 * way * NEAR[j % 2][i]) % n) for j in range(n)]


def along_x(d):
    return [(i, (i // SIDE) * SIDE + (i % SIDE + d) % SIDE) for i in range(SIDE * SIDE)]


def along_y(d):
    return [(i, i + SIDE * d) for i in range(SIDE * (SIDE - d))]


def local(
    query_raw,
    key_raw,
    values,
    out_gate,
    log_decay,
    beta_rate,
    head_gain,
    out_weight,
    residual,
    post_gain,
    router_weight,
    routes,
    placement,
    expert_in,
    expert_out,
):
    n_exp = lax.axis_size("exp")
    experts = router_weight.shape[1]
    at_exp = lax.axis_index("exp")
    at_x = (lax.axis_index("ctx") % SIDE).reshape(1)
    parity = (at_exp % 2).reshape(1)
    core_pairs = [(i, i ^ 1) for i in range(n_exp)]
    same_core = [list(range(0, n_exp, 2)), list(range(1, n_exp, 2))]

    weight_sib = lax.ppermute(out_weight, "exp", core_pairs)

    g, o, z = delta_local(query_raw, key_raw, values, log_decay, beta_rate)
    near = [lax.ppermute(z, "ctx", along_x(d)) for d in range(1, SIDE)]
    total, prefix = pl.pallas_call(
        fold_kernel,
        grid=(1,),
        out_shape=(jax.ShapeDtypeStruct(z.shape, BF), jax.ShapeDtypeStruct(z.shape, F32)),
        in_specs=[pl.BlockSpec(memory_space=pltpu.SMEM)] + [whole(z.shape)] * 4,
        out_specs=(whole(z.shape), whole(z.shape)),
        compiler_params=params(56),
    )(at_x, z, *near)
    far = [lax.ppermute(total, "ctx", along_y(d)) for d in range(1, SIDE)]
    core_out, mine, sib = core_local(parity, g, o, prefix, far, out_gate, head_gain.reshape(1, K))

    got = lax.ppermute(sib, "exp", core_pairs)
    terms = project(mine, got, out_weight, weight_sib)
    terms, routes = lax.optimization_barrier((terms, routes))
    attn = lax.psum_scatter(
        terms, "exp", scatter_dimension=0, tiled=True, axis_index_groups=same_core
    ).astype(F32)
    routes_all = lax.all_gather(routes, "exp", tiled=True)
    rows = routes_all.shape[0]
    chips = n_exp // 2
    at_z = at_exp // 2
    at_core = at_exp % 2
    shift = jnp.where(
        at_core == 0,
        jnp.asarray(NEAR[0] + NEAR[1] + FAR[0] + FAR[1], jnp.int32),
        jnp.asarray(NEAR[1] + NEAR[0] + FAR[1] + FAR[0], jnp.int32),
    )
    flip = jnp.asarray(([0] * GROUP + [1] * GROUP) * 2, jnp.int32)
    order = 2 * ((at_z + shift) % chips) + (at_core + flip) % 2
    routes_rel = routes_all.reshape(n_exp, TOK, -1)[order].reshape(rows, -1)
    ids = jnp.arange(experts, dtype=jnp.int32)
    chosen = jnp.any(routes_rel[:, :, None] == ids[None, None, :], axis=1)
    wide = n_exp * GROUP * CAP
    lanes = jnp.arange(wide, dtype=jnp.int32)
    holder = (lanes // (GROUP * CAP)) * n_exp + at_exp
    spread = (placement[:, None] == holder[None, :]).astype(BF)
    named = jnp.dot(chosen.astype(BF), spread, preferred_element_type=F32)
    step = jnp.arange(TOK, dtype=jnp.int32)
    before = (step[:, None] > step[None, :]).astype(BF)
    rank = jnp.einsum(
        "ts,bsl->btl",
        before,
        named.astype(BF).reshape(rows // TOK, TOK, wide),
        preferred_element_type=F32,
    ).reshape(rows, wide)
    block = (jnp.arange(rows, dtype=jnp.int32) // TOK) % GROUP
    sel = (
        (named > 0.5)
        & (rank == (lanes % CAP).astype(F32)[None, :])
        & (block[:, None] == ((lanes // CAP) % GROUP)[None, :])
    )
    picks = sel.astype(BF)
    half_rows = rows // 2
    attn, picks, chosen = lax.optimization_barrier((attn, picks, chosen))
    mid = lax.optimization_barrier((residual.astype(F32) + attn).astype(BF)).astype(F32)
    normed = (mid / jnp.sqrt(jnp.mean(mid * mid, axis=-1, keepdims=True) + EPS) * post_gain).astype(
        BF
    )
    around = [lax.ppermute(normed, "exp", along_z(i, -1, n_exp)) for i in range(1, GROUP)]
    near_mine = jnp.concatenate([normed] + around, 0)
    near_mine, normed = lax.optimization_barrier((near_mine, normed))
    near_sib = lax.ppermute(near_mine, "exp", core_pairs)
    normed_all = lax.all_gather(normed, "exp", tiled=True)

    def spread_out(rows):
        return lax.all_to_all(rows, "ctx", split_axis=0, concat_axis=0, tiled=True)

    def experts_on(rows):
        return expert(rows.reshape(-1, D), expert_in[0], expert_out[0]).reshape(rows.shape)

    near_rows = dispatch_near(picks[:half_rows], near_mine, near_sib)
    near_in = spread_out(near_rows)
    near_in, normed_far = lax.optimization_barrier((near_in, normed_all))
    far_rows = dispatch_far(order[half_rows // TOK :], picks[half_rows:], normed_far)
    far_in = spread_out(far_rows)
    near_out = experts_on(near_in)
    far_out = experts_on(far_in)

    logits = jnp.dot(normed_far, router_weight, preferred_element_type=F32)
    logits = logits.reshape(n_exp, TOK, experts)[order].reshape(rows, experts)
    raised = jnp.where(chosen, jnp.exp(logits), 0.0)
    gates = raised / jnp.sum(raised, axis=-1, keepdims=True)
    mine_gates = jnp.dot(gates, spread.astype(F32), precision=lax.Precision.HIGHEST)
    weights = jnp.where(sel, mine_gates, 0.0).astype(BF)

    far_back = spread_out(far_out)
    near_out, far_back = lax.optimization_barrier((near_out, far_back))
    near_back = spread_out(near_out)

    far_got = lax.ppermute(combine(weights, far_back, 3, 1), "exp", core_pairs)
    far_own = combine(weights, far_back, 2, 0)
    tables = [[GROUP] * chips, [GROUP] * chips]
    for core in range(2):
        for i, d in enumerate(FAR[core]):
            tables[core][d % chips] = i
    table = jnp.where(at_core == 0, *[jnp.asarray(a, jnp.int32) for a in tables])
    at = table[(jnp.arange(chips, dtype=jnp.int32) - at_z) % chips]
    far_sum = lax.psum_scatter(
        place(at, far_own, far_got),
        "exp",
        scatter_dimension=0,
        tiled=True,
        axis_index_groups=same_core,
    )

    near_got = lax.ppermute(combine(weights, near_back, 1, 1), "exp", core_pairs)
    near_own = combine(weights, near_back, 0, 0)
    near_sum = (near_own.astype(F32) + near_got.astype(F32)).reshape(GROUP, TOK, D)
    mixture = near_sum[0] + far_sum.astype(F32)
    for i in (3, 1, 2):
        sent = lax.ppermute(near_sum[i].astype(BF), "exp", along_z(i, 1, n_exp))
        mixture += sent.astype(F32)
    return (core_out, (mid + mixture).astype(BF))


def solution(mesh):
    placed = (
        P("ctx", "exp"),
        P("ctx", "exp"),
        P("ctx", "exp"),
        P("ctx", "exp"),
        P("exp", "ctx"),
        P("exp", "ctx"),
        P(),
        P("exp", None),
        P(("ctx", "exp"), None),
        P(),
        P(),
        P(("ctx", "exp"), None),
        P(),
        P(("ctx", "exp"), None, None),
        P(("ctx", "exp"), None, None),
    )
    return jax.shard_map(
        local,
        mesh=mesh,
        in_specs=placed,
        out_specs=(P("ctx", "exp"), P(("ctx", "exp"), None)),
        check_vma=False,
    )
```

```python
import math

import jax
import jax.numpy as jnp
from jax import lax
from jax.experimental import pallas as pl
from jax.experimental.pallas import tpu as pltpu
from jax.sharding import PartitionSpec as P

F32=jnp.float32; BF=jnp.bfloat16
EPS=1e-6
C=64
K=128
UNROLL = 16

def mm(a,b):
    return lax.dot_general(a,b,(((1,),(0,)),((),())),preferred_element_type=F32)

def split(a):
    hi=a.astype(BF)
    return hi,(a-hi.astype(F32)).astype(BF)

def mm3(a,b):
    ah,al=split(a); bh,bl=split(b)
    n=b.shape[1]
    if n==K:
        r=mm(jnp.concatenate([ah,al],1),jnp.concatenate([jnp.concatenate([bh,bl],1)]*2,0))
        return r[:,:n]+r[:,n:]
    return mm(jnp.concatenate([ah,al],1),jnp.concatenate([bh,bh],0))+mm(ah,bl)

def mm2(a,b):
    bh,bl=split(b)
    return mm(jnp.concatenate([a,a],1),jnp.concatenate([bh,bl],0))

def mm2l(a,b):
    ah,al=split(a)
    return mm(jnp.concatenate([ah,al],1),jnp.concatenate([b,b],0))

def mm1(a,b):
    return mm(a.astype(BF),b.astype(BF))

def delta_kernel(q_ref,k_ref,v_ref,row_ref,col_ref,go_g,go_o,z_out,wq_s,u_s,p_s,kw_s,dr_s,el_s):
    n=q_ref.shape[0]//C
    rows=lax.broadcasted_iota(jnp.int32,(2*C,2*C),0)
    cols=lax.broadcasted_iota(jnp.int32,(2*C,2*C),1)
    same=(rows//C)==(cols//C)
    strict=same&(rows>cols)
    within=same&(rows>=cols)
    lane=lax.broadcasted_iota(jnp.int32,(2*C,128),1)
    half=lax.broadcasted_iota(jnp.int32,(2*C,1),0)<C
    levels=[]
    b=1
    while b<C:
        levels.append(strict&((rows//(2*b))==(cols//(2*b)))&((rows//b)!=(cols//b)))
        b*=2
    def unit(m):
        return m*lax.rsqrt(jnp.sum(m*m,axis=-1,keepdims=True)+EPS)
    def prep(step,carry):
        amat=[];xs=[];rhs=[];kts=[];ids=[]
        allc=col_ref[...]
        for u in range(UNROLL):
            c=step*UNROLL+u
            ids.append(c)
            at=pl.ds(pl.multiple_of(c*C,C),C)
            kb=k_ref[at,:]
            qb=q_ref[at,:]
            k2=jnp.concatenate([kb,kb],0)
            q2=jnp.concatenate([qb,qb],0)
            kt=k2.T
            raw=mm(jnp.concatenate([k2,q2],0),kt)
            kf=k2.astype(F32)
            qf=q2.astype(F32)
            sk=lax.rsqrt(jnp.sum(kf*kf,axis=-1,keepdims=True)+EPS)
            sq=lax.rsqrt(jnp.sum(qf*qf,axis=-1,keepdims=True)+EPS)*(1.0/math.sqrt(K))
            sk_row=lax.rsqrt(jnp.sum(jnp.where(rows==cols,raw[:2*C],0.0),axis=0,keepdims=True)+EPS)
            g_row=row_ref[pl.ds(c,1),:]
            last_row=row_ref[pl.ds(n+c,1),:]
            b_row=row_ref[pl.ds(2*n+c,1),:]
            g_col=jnp.sum(jnp.where(lane==c,allc,0.0),axis=1,keepdims=True)
            b_col=jnp.sum(jnp.where(lane==n+c,allc,0.0),axis=1,keepdims=True)
            l_col=jnp.sum(jnp.where(lane==2*n+c,allc,0.0),axis=1,keepdims=True)
            fall=jnp.exp(jnp.where(within,g_col-g_row,0.0))*sk_row
            a=jnp.where(strict,fall*(b_col*sk)*raw[:2*C],0.0)
            p_s[c]=jnp.where(within,fall*sq*raw[2*C:],0.0).astype(BF)
            eg=jnp.exp(g_col)
            vb=v_ref[at,:]
            v2=jnp.concatenate([vb[:,:K],vb[:,K:]],0)
            rhs.append((b_row*jnp.exp(g_row)*sk_row,b_row,k2,v2))
            wq_s[c,1]=((eg*sq)*qf).astype(BF)
            kts.append((kt,sk*jnp.exp(l_col-g_col)))
            el_s[c]=jnp.exp(last_row)
            amat.append(a)
            xs.append(jnp.where(rows==cols,1.0,0.0)-jnp.where(levels[0],a,0.0))
        for lev in levels[1:]:
            mids=[mm3(jnp.where(lev,a,0.0),x) for a,x in zip(amat,xs)]
            xs=[x-mm3(x,m) for x,m in zip(xs,mids)]
        for c,x,(wr,br,k2,v2),(kt,kc) in zip(ids,xs,rhs,kts):
            w=mm2l(x*wr,k2)
            u=mm2l(x*br,v2)
            wq_s[c,0]=w.astype(BF)
            u_s[c]=u
            wu=jnp.concatenate([w,u],1)*kc
            both=jnp.concatenate([jnp.where(half,wu,0.0),jnp.where(half,0.0,wu)],1)
            td=mm2(kt,both)
            for h in range(2):
                kw_s[h,c]=td[:,h*2*K:h*2*K+K]
                dr_s[h,c]=td[:,h*2*K+K:(h+1)*2*K]
        return carry
    lax.fori_loop(0,n//UNROLL,prep,0)
    eye=jnp.where(lax.broadcasted_iota(jnp.int32,(K,K),0)==lax.broadcasted_iota(jnp.int32,(K,K),1),1.0,0.0)
    start=jnp.concatenate([eye,jnp.zeros((K,K),F32)],1)
    def chain(c,zs):
        new=[];fresh=[];outs=[]
        el=el_s[c]
        for h in range(2):
            z=zs[h]
            zb=z.astype(BF)
            e=jnp.sum(jnp.where(lax.broadcasted_iota(jnp.int32,(1,2*C),1)==h*C,el,0.0),axis=1,keepdims=True)
            t=e*z-mm3(kw_s[h,c],z)
            new.append(jnp.concatenate([t[:,:K],t[:,K:]+dr_s[h,c]],1))
            w=wq_s[c,0,h*C:(h+1)*C,:]
            q=wq_s[c,1,h*C:(h+1)*C,:]
            r=mm(jnp.concatenate([w,q],0),zb)
            f=-r[:C]
            uu=u_s[c,h*C:(h+1)*C,:]
            fresh.append(jnp.concatenate([f[:,:K],f[:,K:]+uu],1))
            outs.append(r[C:])
        out=jnp.concatenate(outs,0)+mm(p_s[c],jnp.concatenate(fresh,0).astype(BF))
        at=pl.ds(pl.multiple_of(c*C,C),C)
        for h in range(2):
            go_g[h,at,:]=out[h*C:(h+1)*C,:K].astype(BF)
            go_o[h,at,:]=out[h*C:(h+1)*C,K:]
        return tuple(new)
    zs=lax.fori_loop(0,n,chain,(start,start),unroll=8)
    for h in range(2):
        z_out[h]=zs[h].astype(BF)

def whole(shape):
    return pl.BlockSpec(tuple(shape),lambda *_: (0,)*len(shape))

def delta_local(q,k,v,ld,beta):
    t=q.shape[0]; n=t//C
    g=jnp.cumsum(ld.reshape(2,n,C),axis=-1)
    last=jnp.broadcast_to(g[:,:,-1:],g.shape)
    pack=lambda a: jnp.transpose(a,(1,0,2)).reshape(n,2*C)
    rate=pack(beta.reshape(2,n,C))
    row=jnp.concatenate([pack(g),pack(last),rate],0)
    col=jnp.concatenate([pack(g).T,rate.T,pack(last).T,jnp.zeros((2*C,128-3*n),F32)],1)
    shapes=[((2,t,K),BF),((2,t,K),F32),((2,K,2*K),BF)]
    return pl.pallas_call(
        delta_kernel,
        grid=(1,),
        out_shape=[jax.ShapeDtypeStruct(a,d) for a,d in shapes],
        in_specs=[whole(a.shape) for a in (q,k,v,row,col)],out_specs=[whole(a) for a,d in shapes],
        scratch_shapes=[pltpu.VMEM((n,2,2*C,K),BF),pltpu.VMEM((n,2*C,K),F32),pltpu.VMEM((n,2*C,2*C),BF),
            pltpu.VMEM((2,n,K,K),F32),pltpu.VMEM((2,n,K,K),F32),pltpu.VMEM((n,1,2*C),F32)],
        compiler_params=pltpu.CompilerParams(vmem_limit_bytes=56*2**20),
    )(q,k,v,row,col)

CAP = 4
GROUP = 4
TOK = 64
SIDE = 4
D = 2048


def params(mib):
    return pltpu.CompilerParams(vmem_limit_bytes=mib * 2**20)


def fold_kernel(x_ref, own, a1, a2, a3, total_ref, prefix_ref):
    x = x_ref[0]
    eye = jnp.where(
        lax.broadcasted_iota(jnp.int32, (K, K), 0) == lax.broadcasted_iota(jnp.int32, (K, K), 1),
        1.0,
        0.0,
    )
    for h in range(2):
        near = [own[h].astype(F32), a1[h].astype(F32), a2[h].astype(F32), a3[h].astype(F32)]
        z = jnp.concatenate([eye, jnp.zeros((K, K), F32)], 1)
        prefix = z
        for j in range(SIDE):
            item = near[0]
            for d in range(1, SIDE):
                item = jnp.where((x - j) % SIDE == d, near[d], item)
            if j == 0:
                z = item
            else:
                zh, zl = split(z)
                m = item[:, :K].astype(BF)
                t = mm(m, zh) + mm(m, zl)
                z = jnp.concatenate([t[:, :K], t[:, K:] + item[:, K:]], 1)
            if j < SIDE - 1:
                prefix = jnp.where(x == j + 1, z, prefix)
        total_ref[h] = z.astype(BF)
        prefix_ref[h] = prefix


def core_kernel(
    par_ref, g_ref, o_ref, prefix, b1, b2, b3, gate_ref, gain_ref, core_ref, mine, sib, state
):
    gain = gain_ref[...]
    even = par_ref[0] == 0

    @pl.when(pl.program_id(0) == 0)
    def _():
        for h in range(2):
            e = b3[h][:, K:].astype(F32)
            for b in (b2, b1):
                eh, el = split(e)
                m = b[h][:, :K]
                e = mm(m, eh) + mm(m, el) + b[h][:, K:].astype(F32)
            e = mm3(prefix[h][:, :K], e) + prefix[h][:, K:]
            eh, el = split(e)
            state[h] = jnp.concatenate([eh, el], 1)

    step = 2 * TOK
    for i in range(g_ref.shape[1] // step):
        at = slice(i * step, (i + 1) * step)
        outs = []
        for h in range(2):
            both = mm(g_ref[h, at, :], state[h])
            core = o_ref[h, at, :] + both[:, :K] + both[:, K:]
            gate = gate_ref[at, h * K : (h + 1) * K].astype(F32)
            scaled = core * lax.rsqrt(jnp.mean(core * core, axis=-1, keepdims=True) + EPS)
            outs.append((scaled * gain * (gate / (1.0 + jnp.exp(-gate)))).astype(BF))
        out = jnp.concatenate(outs, 1)
        core_ref[at, :] = out
        to = slice(i * TOK, (i + 1) * TOK)
        mine[to, :] = jnp.where(even, out[:TOK], out[TOK:])
        sib[to, :] = jnp.where(even, out[TOK:], out[:TOK])


def core_local(parity, g, o, prefix, far, gate, gain):
    rows, wide = gate.shape
    part = 512
    half = jax.ShapeDtypeStruct((rows // 2, wide), BF)
    heads = pl.BlockSpec((2, part, K), lambda i: (0, i, 0))
    half_spec = pl.BlockSpec((part // 2, wide), lambda i: (i, 0))
    full_spec = pl.BlockSpec((part, wide), lambda i: (i, 0))
    return pl.pallas_call(
        core_kernel,
        grid=(rows // part,),
        out_shape=(jax.ShapeDtypeStruct(gate.shape, BF), half, half),
        in_specs=[pl.BlockSpec(memory_space=pltpu.SMEM), heads, heads]
        + [whole(prefix.shape)] * 4
        + [full_spec, whole(gain.shape)],
        out_specs=(full_spec, half_spec, half_spec),
        scratch_shapes=[pltpu.VMEM((2, K, 2 * K), BF)],
        compiler_params=params(56),
    )(parity, g, o, prefix, *far, gate, gain)


def project_kernel(a_ref, b_ref, wa_ref, wb_ref, out_ref):
    out_ref[...] = (mm(a_ref[...], wa_ref[...]) + mm(b_ref[...], wb_ref[...])).astype(BF)


def project(a, b, wa, wb):
    rows, depth = a.shape
    wide = 512
    return pl.pallas_call(
        project_kernel,
        grid=(D // wide,),
        out_shape=jax.ShapeDtypeStruct((rows, D), BF),
        in_specs=[
            pl.BlockSpec((rows, depth), lambda i: (0, 0)),
            pl.BlockSpec((rows, depth), lambda i: (0, 0)),
            pl.BlockSpec((depth, wide), lambda i: (0, i)),
            pl.BlockSpec((depth, wide), lambda i: (0, i)),
        ],
        out_specs=pl.BlockSpec((rows, wide), lambda i: (0, i)),
        compiler_params=params(16),
    )(a, b, wa, wb)


def pick(sel, rows):
    out = lax.dot_general(sel, rows, (((0,), (0,)), ((), ())), preferred_element_type=F32)
    return out.astype(BF).reshape(sel.shape[1] // (GROUP * CAP), GROUP * CAP, D)


def near_kernel(sel_ref, mine_ref, sib_ref, out_ref):
    out_ref[:, : GROUP * CAP, :] = pick(sel_ref[: GROUP * TOK], mine_ref[...])
    out_ref[:, GROUP * CAP :, :] = pick(sel_ref[GROUP * TOK :], sib_ref[...])


def dispatch_near(sel, mine, sib):
    return pl.pallas_call(
        near_kernel,
        grid=(1,),
        out_shape=jax.ShapeDtypeStruct((16, 2 * GROUP * CAP, D), BF),
        in_specs=[whole(sel.shape), whole(mine.shape), whole(sib.shape)],
        out_specs=whole((16, 2 * GROUP * CAP, D)),
        compiler_params=params(16),
    )(sel, mine, sib)


def far_kernel(order_ref, sel_ref, r0, r1, r2, r3, out_ref):
    rows = jnp.concatenate([r0[...], r1[...], r2[...], r3[...]], 0)
    out_ref[...] = pick(sel_ref[...], rows)


def dispatch_far(order, sel, rows):
    part = GROUP * TOK

    def block(j):
        return pl.BlockSpec((TOK, D), lambda g, order: (order[GROUP * g + j], 0))

    return pl.pallas_call(
        far_kernel,
        grid_spec=pltpu.PrefetchScalarGridSpec(
            num_scalar_prefetch=1,
            grid=(2,),
            in_specs=[pl.BlockSpec((part, sel.shape[1]), lambda g, order: (g, 0))]
            + [block(j) for j in range(GROUP)],
            out_specs=pl.BlockSpec((16, GROUP * CAP, D), lambda g, order: (0, g, 0)),
        ),
        out_shape=jax.ShapeDtypeStruct((16, 2 * GROUP * CAP, D), BF),
        compiler_params=params(16),
    )(order, sel, rows, rows, rows, rows)


def expert_kernel(x_ref, gate_ref, up_ref, down_ref, out_ref, total):
    x = x_ref[...]
    gate = mm(x, gate_ref[...])
    act = (gate / (1.0 + jnp.exp(-gate)) * mm(x, up_ref[...])).astype(BF)
    term = mm(act, down_ref[...])
    step = pl.program_id(0)

    @pl.when(step == 0)
    def _():
        total[...] = term

    @pl.when(step > 0)
    def _():
        out_ref[...] = (total[...] + term).astype(BF)


def expert(x, gate_up, down):
    part = down.shape[0] // 2
    return pl.pallas_call(
        expert_kernel,
        grid=(2,),
        out_shape=jax.ShapeDtypeStruct(x.shape, BF),
        in_specs=[
            whole(x.shape),
            pl.BlockSpec((D, part), lambda i: (0, i)),
            pl.BlockSpec((D, part), lambda i: (0, 2 + i)),
            pl.BlockSpec((part, D), lambda i: (i, 0)),
        ],
        out_specs=whole(x.shape),
        scratch_shapes=[pltpu.VMEM(x.shape, F32)],
        cost_estimate=pl.CostEstimate(
            flops=6 * x.shape[0] * D * down.shape[0], bytes_accessed=10 * 2**20, transcendentals=0
        ),
        compiler_params=params(32),
    )(x, gate_up, gate_up, down)


def combine_kernel(w_ref, y_ref, out_ref):
    rows = y_ref[...].reshape(w_ref.shape[1], D)
    out_ref[...] = mm(w_ref[...], rows).astype(BF)


def combine(weights, y, half):
    part = GROUP * TOK
    return pl.pallas_call(
        combine_kernel,
        grid=(1,),
        out_shape=jax.ShapeDtypeStruct((part, D), BF),
        in_specs=[
            whole(weights.shape),
            pl.BlockSpec((y.shape[0], GROUP * CAP, D), lambda i: (0, half, 0)),
        ],
        out_specs=whole((part, D)),
        compiler_params=params(16),
    )(weights, y)


def place_kernel(at_ref, own_ref, got_ref, out_ref):
    out_ref[...] = jnp.zeros_like(out_ref)
    for i in range(GROUP):
        rows = slice(i * TOK, (i + 1) * TOK)
        total = own_ref[rows, :].astype(F32) + got_ref[rows, :].astype(F32)
        out_ref[pl.ds(pl.multiple_of(at_ref[i] * TOK, TOK), TOK), :] = total.astype(BF)


def place(at, own, got, chips):
    return pl.pallas_call(
        place_kernel,
        grid=(1,),
        in_specs=[pl.BlockSpec(memory_space=pltpu.SMEM), whole(own.shape), whole(got.shape)],
        out_specs=whole((chips * TOK, D)),
        out_shape=jax.ShapeDtypeStruct((chips * TOK, D), BF),
        compiler_params=params(16),
    )(at, own, got)


NEAR = ((0, 1, -1, 2), (0, 1, -1, -2))
FAR = ((-2, 3, -3, 4), (2, 3, -3, 4))


def along_z(i, way, n):
    return [(j, (j + 2 * way * NEAR[j % 2][i]) % n) for j in range(n)]


def along_x(d):
    return [(i, (i // SIDE) * SIDE + (i % SIDE + d) % SIDE) for i in range(SIDE * SIDE)]


def along_y(d):
    return [(i, i + SIDE * d) for i in range(SIDE * (SIDE - d))]


def local(
    query_raw,
    key_raw,
    values,
    out_gate,
    log_decay,
    beta_rate,
    head_gain,
    out_weight,
    residual,
    post_gain,
    router_weight,
    routes,
    placement,
    expert_in,
    expert_out,
):
    n_exp = lax.axis_size("exp")
    experts = router_weight.shape[1]
    at_exp = lax.axis_index("exp")
    at_x = (lax.axis_index("ctx") % SIDE).reshape(1)
    parity = (at_exp % 2).reshape(1)
    core_pairs = [(i, i ^ 1) for i in range(n_exp)]
    same_core = [list(range(0, n_exp, 2)), list(range(1, n_exp, 2))]

    weight_sib = lax.ppermute(out_weight, "exp", core_pairs)

    g, o, z = delta_local(query_raw, key_raw, values, log_decay, beta_rate)
    near = [lax.ppermute(z, "ctx", along_x(d)) for d in range(1, SIDE)]
    total, prefix = pl.pallas_call(
        fold_kernel,
        grid=(1,),
        out_shape=(jax.ShapeDtypeStruct(z.shape, BF), jax.ShapeDtypeStruct(z.shape, F32)),
        in_specs=[pl.BlockSpec(memory_space=pltpu.SMEM)] + [whole(z.shape)] * 4,
        out_specs=(whole(z.shape), whole(z.shape)),
        compiler_params=params(56),
    )(at_x, z, *near)
    far = [lax.ppermute(total, "ctx", along_y(d)) for d in range(1, SIDE)]
    core_out, mine, sib = core_local(parity, g, o, prefix, far, out_gate, head_gain.reshape(1, K))

    got = lax.ppermute(sib, "exp", core_pairs)
    terms = project(mine, got, out_weight, weight_sib)
    terms, routes = lax.optimization_barrier((terms, routes))
    attn = lax.psum_scatter(
        terms, "exp", scatter_dimension=0, tiled=True, axis_index_groups=same_core
    ).astype(F32)
    routes_all = lax.all_gather(routes, "exp", tiled=True)
    rows = routes_all.shape[0]
    chips = n_exp // 2
    at_z = at_exp // 2
    at_core = at_exp % 2
    shift = jnp.where(
        at_core == 0,
        jnp.asarray(NEAR[0] + NEAR[1] + FAR[0] + FAR[1], jnp.int32),
        jnp.asarray(NEAR[1] + NEAR[0] + FAR[1] + FAR[0], jnp.int32),
    )
    flip = jnp.asarray(([0] * GROUP + [1] * GROUP) * 2, jnp.int32)
    order = 2 * ((at_z + shift) % chips) + (at_core + flip) % 2
    routes_rel = routes_all.reshape(n_exp, TOK, -1)[order].reshape(rows, -1)
    ids = jnp.arange(experts, dtype=jnp.int32)
    chosen = jnp.any(routes_rel[:, :, None] == ids[None, None, :], axis=1)
    wide = n_exp * GROUP * CAP
    lanes = jnp.arange(wide, dtype=jnp.int32)
    holder = (lanes // (GROUP * CAP)) * n_exp + at_exp
    spread = (placement[:, None] == holder[None, :]).astype(BF)
    named = jnp.dot(chosen.astype(BF), spread, preferred_element_type=F32)
    step = jnp.arange(TOK, dtype=jnp.int32)
    before = (step[:, None] > step[None, :]).astype(BF)
    rank = jnp.einsum(
        "ts,bsl->btl",
        before,
        named.astype(BF).reshape(rows // TOK, TOK, wide),
        preferred_element_type=F32,
    ).reshape(rows, wide)
    block = (jnp.arange(rows, dtype=jnp.int32) // TOK) % GROUP
    sel = (
        (named > 0.5)
        & (rank == (lanes % CAP).astype(F32)[None, :])
        & (block[:, None] == ((lanes // CAP) % GROUP)[None, :])
    )
    picks = sel.astype(BF)
    half_rows = rows // 2
    far_order = order[rows // TOK // 2 :]
    attn, picks, chosen, far_order = lax.optimization_barrier((attn, picks, chosen, far_order))
    mid = lax.optimization_barrier((residual.astype(F32) + attn).astype(BF)).astype(F32)
    normed = (mid / jnp.sqrt(jnp.mean(mid * mid, axis=-1, keepdims=True) + EPS) * post_gain).astype(
        BF
    )
    around = [lax.ppermute(normed, "exp", along_z(i, -1, n_exp)) for i in range(1, GROUP)]
    near_mine = jnp.concatenate([normed] + around, 0)
    near_sib = lax.ppermute(near_mine, "exp", core_pairs)
    normed_all = lax.all_gather(normed, "exp", tiled=True)

    def spread_out(rows):
        return lax.all_to_all(rows, "ctx", split_axis=0, concat_axis=0, tiled=True)

    def experts_on(rows):
        return expert(rows.reshape(-1, D), expert_in[0], expert_out[0]).reshape(rows.shape)

    near_rows = dispatch_near(picks[:half_rows], near_mine, near_sib)
    near_in = spread_out(near_rows)
    near_in, normed_far = lax.optimization_barrier((near_in, normed_all))
    far_rows = dispatch_far(far_order, picks[half_rows:], normed_far)
    far_in = spread_out(far_rows)
    near_out = experts_on(near_in)
    far_out = experts_on(far_in)

    logits = jnp.dot(normed_far, router_weight, preferred_element_type=F32)
    logits = logits.reshape(n_exp, TOK, experts)[order].reshape(rows, experts)
    raised = jnp.where(chosen, jnp.exp(logits), 0.0)
    gates = raised / jnp.sum(raised, axis=-1, keepdims=True)
    mine_gates = jnp.dot(gates, spread.astype(F32), precision=lax.Precision.HIGHEST)
    weights = jnp.where(sel, mine_gates, 0.0).astype(BF).reshape(4, rows // 4, wide)
    weights = lax.optimization_barrier([weights[i] for i in range(4)])

    far_back = spread_out(far_out)
    near_out, far_back = lax.optimization_barrier((near_out, far_back))

    far_got = lax.ppermute(combine(weights[3], far_back, 1), "exp", core_pairs)
    far_own = combine(weights[2], far_back, 0)
    far_shift = jnp.where(at_core == 0, *[jnp.asarray(a, jnp.int32) for a in FAR])
    far_placed = place((at_z + far_shift + chips) % chips, far_own, far_got, chips)
    near_out, far_placed = lax.optimization_barrier((near_out, far_placed))
    near_back = spread_out(near_out)
    far_sum = lax.psum_scatter(
        far_placed, "exp", scatter_dimension=0, tiled=True, axis_index_groups=same_core
    )

    near_got = lax.ppermute(combine(weights[1], near_back, 1), "exp", core_pairs)
    near_own = combine(weights[0], near_back, 0)
    near_sum = (near_own.astype(F32) + near_got.astype(F32)).reshape(GROUP, TOK, D)
    mixture = near_sum[0] + far_sum.astype(F32)
    for i in (3, 1, 2):
        sent = lax.ppermute(near_sum[i].astype(BF), "exp", along_z(i, 1, n_exp))
        mixture += sent.astype(F32)
    return (core_out, (mid + mixture).astype(BF))


def solution(mesh):
    placed = (
        P("ctx", "exp"),
        P("ctx", "exp"),
        P("ctx", "exp"),
        P("ctx", "exp"),
        P("exp", "ctx"),
        P("exp", "ctx"),
        P(),
        P("exp", None),
        P(("ctx", "exp"), None),
        P(),
        P(),
        P(("ctx", "exp"), None),
        P(),
        P(("ctx", "exp"), None, None),
        P(("ctx", "exp"), None, None),
    )
    return jax.shard_map(
        local,
        mesh=mesh,
        in_specs=placed,
        out_specs=(P("ctx", "exp"), P(("ctx", "exp"), None)),
        check_vma=False,
    )
```

```python
import math

import jax
import jax.numpy as jnp
from jax import lax
from jax.experimental import pallas as pl
from jax.experimental.pallas import tpu as pltpu
from jax.sharding import PartitionSpec as P

F32=jnp.float32; BF=jnp.bfloat16
EPS=1e-6
C=64
K=128
UNROLL = 16

def mm(a,b):
    return lax.dot_general(a,b,(((1,),(0,)),((),())),preferred_element_type=F32)

def split(a):
    hi=a.astype(BF)
    return hi,(a-hi.astype(F32)).astype(BF)

def mm3(a,b):
    ah,al=split(a); bh,bl=split(b)
    n=b.shape[1]
    if n==K:
        r=mm(jnp.concatenate([ah,al],1),jnp.concatenate([jnp.concatenate([bh,bl],1)]*2,0))
        return r[:,:n]+r[:,n:]
    return mm(jnp.concatenate([ah,al],1),jnp.concatenate([bh,bh],0))+mm(ah,bl)

def mm2(a,b):
    bh,bl=split(b)
    return mm(jnp.concatenate([a,a],1),jnp.concatenate([bh,bl],0))

def mm2l(a,b):
    ah,al=split(a)
    return mm(jnp.concatenate([ah,al],1),jnp.concatenate([b,b],0))

def mm1(a,b):
    return mm(a.astype(BF),b.astype(BF))

def delta_kernel(q_ref,k_ref,v_ref,row_ref,col_ref,go_g,go_o,z_out,wq_s,u_s,p_s,kw_s,dr_s,el_s):
    n=q_ref.shape[0]//C
    rows=lax.broadcasted_iota(jnp.int32,(2*C,2*C),0)
    cols=lax.broadcasted_iota(jnp.int32,(2*C,2*C),1)
    same=(rows//C)==(cols//C)
    strict=same&(rows>cols)
    within=same&(rows>=cols)
    lane=lax.broadcasted_iota(jnp.int32,(2*C,128),1)
    half=lax.broadcasted_iota(jnp.int32,(2*C,1),0)<C
    levels=[]
    b=1
    while b<C:
        levels.append(strict&((rows//(2*b))==(cols//(2*b)))&((rows//b)!=(cols//b)))
        b*=2
    def unit(m):
        return m*lax.rsqrt(jnp.sum(m*m,axis=-1,keepdims=True)+EPS)
    def prep(step,carry):
        amat=[];xs=[];rhs=[];kts=[];ids=[]
        allc=col_ref[...]
        for u in range(UNROLL):
            c=step*UNROLL+u
            ids.append(c)
            at=pl.ds(pl.multiple_of(c*C,C),C)
            kb=k_ref[at,:]
            qb=q_ref[at,:]
            k2=jnp.concatenate([kb,kb],0)
            q2=jnp.concatenate([qb,qb],0)
            kt=k2.T
            raw=mm(jnp.concatenate([k2,q2],0),kt)
            kf=k2.astype(F32)
            qf=q2.astype(F32)
            sk=lax.rsqrt(jnp.sum(kf*kf,axis=-1,keepdims=True)+EPS)
            sq=lax.rsqrt(jnp.sum(qf*qf,axis=-1,keepdims=True)+EPS)*(1.0/math.sqrt(K))
            sk_row=lax.rsqrt(jnp.sum(jnp.where(rows==cols,raw[:2*C],0.0),axis=0,keepdims=True)+EPS)
            g_row=row_ref[pl.ds(c,1),:]
            last_row=row_ref[pl.ds(n+c,1),:]
            b_row=row_ref[pl.ds(2*n+c,1),:]
            g_col=jnp.sum(jnp.where(lane==c,allc,0.0),axis=1,keepdims=True)
            b_col=jnp.sum(jnp.where(lane==n+c,allc,0.0),axis=1,keepdims=True)
            l_col=jnp.sum(jnp.where(lane==2*n+c,allc,0.0),axis=1,keepdims=True)
            fall=jnp.exp(jnp.where(within,g_col-g_row,0.0))*sk_row
            a=jnp.where(strict,fall*(b_col*sk)*raw[:2*C],0.0)
            p_s[c]=jnp.where(within,fall*sq*raw[2*C:],0.0).astype(BF)
            eg=jnp.exp(g_col)
            vb=v_ref[at,:]
            v2=jnp.concatenate([vb[:,:K],vb[:,K:]],0)
            rhs.append((b_row*jnp.exp(g_row)*sk_row,b_row,k2,v2))
            wq_s[c,1]=((eg*sq)*qf).astype(BF)
            kts.append((kt,sk*jnp.exp(l_col-g_col)))
            el_s[c]=jnp.exp(last_row)
            amat.append(a)
            xs.append(jnp.where(rows==cols,1.0,0.0)-jnp.where(levels[0],a,0.0))
        for lev in levels[1:]:
            mids=[mm3(jnp.where(lev,a,0.0),x) for a,x in zip(amat,xs)]
            xs=[x-mm3(x,m) for x,m in zip(xs,mids)]
        for c,x,(wr,br,k2,v2),(kt,kc) in zip(ids,xs,rhs,kts):
            w=mm2l(x*wr,k2)
            u=mm2l(x*br,v2)
            wq_s[c,0]=w.astype(BF)
            u_s[c]=u
            wu=jnp.concatenate([w,u],1)*kc
            both=jnp.concatenate([jnp.where(half,wu,0.0),jnp.where(half,0.0,wu)],1)
            td=mm2(kt,both)
            for h in range(2):
                kw_s[h,c]=td[:,h*2*K:h*2*K+K]
                dr_s[h,c]=td[:,h*2*K+K:(h+1)*2*K]
        return carry
    lax.fori_loop(0,n//UNROLL,prep,0)
    eye=jnp.where(lax.broadcasted_iota(jnp.int32,(K,K),0)==lax.broadcasted_iota(jnp.int32,(K,K),1),1.0,0.0)
    start=jnp.concatenate([eye,jnp.zeros((K,K),F32)],1)
    def chain(c,zs):
        new=[];fresh=[];outs=[]
        el=el_s[c]
        for h in range(2):
            z=zs[h]
            zb=z.astype(BF)
            e=jnp.sum(jnp.where(lax.broadcasted_iota(jnp.int32,(1,2*C),1)==h*C,el,0.0),axis=1,keepdims=True)
            t=e*z-mm3(kw_s[h,c],z)
            new.append(jnp.concatenate([t[:,:K],t[:,K:]+dr_s[h,c]],1))
            w=wq_s[c,0,h*C:(h+1)*C,:]
            q=wq_s[c,1,h*C:(h+1)*C,:]
            r=mm(jnp.concatenate([w,q],0),zb)
            f=-r[:C]
            uu=u_s[c,h*C:(h+1)*C,:]
            fresh.append(jnp.concatenate([f[:,:K],f[:,K:]+uu],1))
            outs.append(r[C:])
        out=jnp.concatenate(outs,0)+mm(p_s[c],jnp.concatenate(fresh,0).astype(BF))
        at=pl.ds(pl.multiple_of(c*C,C),C)
        for h in range(2):
            go_g[h,at,:]=out[h*C:(h+1)*C,:K].astype(BF)
            go_o[h,at,:]=out[h*C:(h+1)*C,K:]
        return tuple(new)
    zs=lax.fori_loop(0,n,chain,(start,start),unroll=8)
    for h in range(2):
        z_out[h]=zs[h].astype(BF)

def whole(shape):
    return pl.BlockSpec(tuple(shape),lambda *_: (0,)*len(shape))

def delta_local(q,k,v,ld,beta):
    t=q.shape[0]; n=t//C
    g=jnp.cumsum(ld.reshape(2,n,C),axis=-1)
    last=jnp.broadcast_to(g[:,:,-1:],g.shape)
    pack=lambda a: jnp.transpose(a,(1,0,2)).reshape(n,2*C)
    rate=pack(beta.reshape(2,n,C))
    row=jnp.concatenate([pack(g),pack(last),rate],0)
    col=jnp.concatenate([pack(g).T,rate.T,pack(last).T,jnp.zeros((2*C,128-3*n),F32)],1)
    shapes=[((2,t,K),BF),((2,t,K),F32),((2,K,2*K),BF)]
    return pl.pallas_call(
        delta_kernel,
        grid=(1,),
        out_shape=[jax.ShapeDtypeStruct(a,d) for a,d in shapes],
        in_specs=[whole(a.shape) for a in (q,k,v,row,col)],out_specs=[whole(a) for a,d in shapes],
        scratch_shapes=[pltpu.VMEM((n,2,2*C,K),BF),pltpu.VMEM((n,2*C,K),F32),pltpu.VMEM((n,2*C,2*C),BF),
            pltpu.VMEM((2,n,K,K),F32),pltpu.VMEM((2,n,K,K),F32),pltpu.VMEM((n,1,2*C),F32)],
        compiler_params=pltpu.CompilerParams(vmem_limit_bytes=56*2**20),
    )(q,k,v,row,col)

CAP = 4
GROUP = 4
TOK = 64
SIDE = 4
D = 2048


def params(mib):
    return pltpu.CompilerParams(vmem_limit_bytes=mib * 2**20)


def fold_kernel(x_ref, own, a1, a2, a3, total_ref, prefix_ref):
    x = x_ref[0]
    eye = jnp.where(
        lax.broadcasted_iota(jnp.int32, (K, K), 0) == lax.broadcasted_iota(jnp.int32, (K, K), 1),
        1.0,
        0.0,
    )
    for h in range(2):
        near = [own[h].astype(F32), a1[h].astype(F32), a2[h].astype(F32), a3[h].astype(F32)]
        z = jnp.concatenate([eye, jnp.zeros((K, K), F32)], 1)
        prefix = z
        for j in range(SIDE):
            item = near[0]
            for d in range(1, SIDE):
                item = jnp.where((x - j) % SIDE == d, near[d], item)
            if j == 0:
                z = item
            else:
                zh, zl = split(z)
                m = item[:, :K].astype(BF)
                t = mm(m, zh) + mm(m, zl)
                z = jnp.concatenate([t[:, :K], t[:, K:] + item[:, K:]], 1)
            if j < SIDE - 1:
                prefix = jnp.where(x == j + 1, z, prefix)
        total_ref[h] = z.astype(BF)
        prefix_ref[h] = prefix


def core_kernel(
    par_ref, g_ref, o_ref, prefix, b1, b2, b3, gate_ref, gain_ref, core_ref, mine, sib, state
):
    gain = gain_ref[...]
    even = par_ref[0] == 0

    @pl.when(pl.program_id(0) == 0)
    def _():
        for h in range(2):
            e = b3[h][:, K:].astype(F32)
            for b in (b2, b1):
                eh, el = split(e)
                m = b[h][:, :K]
                e = mm(m, eh) + mm(m, el) + b[h][:, K:].astype(F32)
            e = mm3(prefix[h][:, :K], e) + prefix[h][:, K:]
            eh, el = split(e)
            state[h] = jnp.concatenate([eh, el], 1)

    step = 2 * TOK
    for i in range(g_ref.shape[1] // step):
        at = slice(i * step, (i + 1) * step)
        outs = []
        for h in range(2):
            both = mm(g_ref[h, at, :], state[h])
            core = o_ref[h, at, :] + both[:, :K] + both[:, K:]
            gate = gate_ref[at, h * K : (h + 1) * K].astype(F32)
            scaled = core * lax.rsqrt(jnp.mean(core * core, axis=-1, keepdims=True) + EPS)
            outs.append((scaled * gain * (gate / (1.0 + jnp.exp(-gate)))).astype(BF))
        out = jnp.concatenate(outs, 1)
        core_ref[at, :] = out
        to = slice(i * TOK, (i + 1) * TOK)
        mine[to, :] = jnp.where(even, out[:TOK], out[TOK:])
        sib[to, :] = jnp.where(even, out[TOK:], out[:TOK])


def core_local(parity, g, o, prefix, far, gate, gain):
    rows, wide = gate.shape
    part = 512
    half = jax.ShapeDtypeStruct((rows // 2, wide), BF)
    heads = pl.BlockSpec((2, part, K), lambda i: (0, i, 0))
    half_spec = pl.BlockSpec((part // 2, wide), lambda i: (i, 0))
    full_spec = pl.BlockSpec((part, wide), lambda i: (i, 0))
    return pl.pallas_call(
        core_kernel,
        grid=(rows // part,),
        out_shape=(jax.ShapeDtypeStruct(gate.shape, BF), half, half),
        in_specs=[pl.BlockSpec(memory_space=pltpu.SMEM), heads, heads]
        + [whole(prefix.shape)] * 4
        + [full_spec, whole(gain.shape)],
        out_specs=(full_spec, half_spec, half_spec),
        scratch_shapes=[pltpu.VMEM((2, K, 2 * K), BF)],
        compiler_params=params(56),
    )(parity, g, o, prefix, *far, gate, gain)


def project_kernel(a_ref, b_ref, wa_ref, wb_ref, out_ref):
    out_ref[...] = (mm(a_ref[...], wa_ref[...]) + mm(b_ref[...], wb_ref[...])).astype(BF)


def project(a, b, wa, wb):
    rows, depth = a.shape
    wide = 512
    return pl.pallas_call(
        project_kernel,
        grid=(D // wide,),
        out_shape=jax.ShapeDtypeStruct((rows, D), BF),
        in_specs=[
            pl.BlockSpec((rows, depth), lambda i: (0, 0)),
            pl.BlockSpec((rows, depth), lambda i: (0, 0)),
            pl.BlockSpec((depth, wide), lambda i: (0, i)),
            pl.BlockSpec((depth, wide), lambda i: (0, i)),
        ],
        out_specs=pl.BlockSpec((rows, wide), lambda i: (0, i)),
        compiler_params=params(16),
    )(a, b, wa, wb)


def norm_kernel(res_ref, attn_ref, gain_ref, mid_ref, normed_ref):
    mid = (res_ref[...].astype(F32) + attn_ref[...].astype(F32)).astype(BF)
    mid_ref[...] = mid
    mid = mid.astype(F32)
    scale = lax.rsqrt(jnp.mean(mid * mid, axis=-1, keepdims=True) + EPS)
    normed_ref[...] = (mid * scale * gain_ref[...]).astype(BF)


def norm_rows(residual, attn, gain):
    spec = whole(residual.shape)
    shape = jax.ShapeDtypeStruct(residual.shape, BF)
    return pl.pallas_call(
        norm_kernel,
        grid=(1,),
        out_shape=(shape, shape),
        in_specs=[spec, spec, whole(gain.shape)],
        out_specs=(spec, spec),
        compiler_params=params(16),
    )(residual, attn, gain)


def pick(sel, rows):
    out = lax.dot_general(sel, rows, (((0,), (0,)), ((), ())), preferred_element_type=F32)
    return out.astype(BF).reshape(sel.shape[1] // (GROUP * CAP), GROUP * CAP, D)


def near_kernel(sel_ref, *refs):
    *parts, out_ref = refs
    mine = jnp.concatenate([a[...] for a in parts[:GROUP]], 0)
    sib = jnp.concatenate([a[...] for a in parts[GROUP:]], 0)
    out_ref[:, : GROUP * CAP, :] = pick(sel_ref[: GROUP * TOK], mine)
    out_ref[:, GROUP * CAP :, :] = pick(sel_ref[GROUP * TOK :], sib)


def dispatch_near(sel, *parts):
    return pl.pallas_call(
        near_kernel,
        grid=(1,),
        out_shape=jax.ShapeDtypeStruct((16, 2 * GROUP * CAP, D), BF),
        in_specs=[whole(sel.shape)] + [whole(a.shape) for a in parts],
        out_specs=whole((16, 2 * GROUP * CAP, D)),
        compiler_params=params(16),
    )(sel, *parts)


def far_kernel(order_ref, sel_ref, r0, r1, r2, r3, out_ref):
    rows = jnp.concatenate([r0[...], r1[...], r2[...], r3[...]], 0)
    out_ref[...] = pick(sel_ref[...], rows)


def dispatch_far(order, sel, rows):
    part = GROUP * TOK

    def block(j):
        return pl.BlockSpec((TOK, D), lambda g, order: (order[GROUP * g + j], 0))

    return pl.pallas_call(
        far_kernel,
        grid_spec=pltpu.PrefetchScalarGridSpec(
            num_scalar_prefetch=1,
            grid=(2,),
            in_specs=[pl.BlockSpec((part, sel.shape[1]), lambda g, order: (g, 0))]
            + [block(j) for j in range(GROUP)],
            out_specs=pl.BlockSpec((16, GROUP * CAP, D), lambda g, order: (0, g, 0)),
        ),
        out_shape=jax.ShapeDtypeStruct((16, 2 * GROUP * CAP, D), BF),
        compiler_params=params(16),
    )(order, sel, rows, rows, rows, rows)


def expert_kernel(x_ref, gate_ref, up_ref, down_ref, out_ref, total):
    x = x_ref[...]
    gate = mm(x, gate_ref[...])
    act = (gate / (1.0 + jnp.exp(-gate)) * mm(x, up_ref[...])).astype(BF)
    term = mm(act, down_ref[...])
    step = pl.program_id(0)

    @pl.when(step == 0)
    def _():
        total[...] = term

    @pl.when(step > 0)
    def _():
        out_ref[...] = (total[...] + term).astype(BF)


def expert(x, gate_up, down):
    part = down.shape[0] // 2
    return pl.pallas_call(
        expert_kernel,
        grid=(2,),
        out_shape=jax.ShapeDtypeStruct(x.shape, BF),
        in_specs=[
            whole(x.shape),
            pl.BlockSpec((D, part), lambda i: (0, i)),
            pl.BlockSpec((D, part), lambda i: (0, 2 + i)),
            pl.BlockSpec((part, D), lambda i: (i, 0)),
        ],
        out_specs=whole(x.shape),
        scratch_shapes=[pltpu.VMEM(x.shape, F32)],
        cost_estimate=pl.CostEstimate(
            flops=6 * x.shape[0] * D * down.shape[0], bytes_accessed=10 * 2**20, transcendentals=0
        ),
        compiler_params=params(32),
    )(x, gate_up, gate_up, down)


def combine_kernel(w_ref, y_ref, out_ref):
    rows = y_ref[...].reshape(w_ref.shape[1], D)
    out_ref[...] = mm(w_ref[...], rows).astype(BF)


def combine(weights, y, half):
    part = GROUP * TOK
    return pl.pallas_call(
        combine_kernel,
        grid=(1,),
        out_shape=jax.ShapeDtypeStruct((part, D), BF),
        in_specs=[
            whole(weights.shape),
            pl.BlockSpec((y.shape[0], GROUP * CAP, D), lambda i: (0, half, 0)),
        ],
        out_specs=whole((part, D)),
        compiler_params=params(16),
    )(weights, y)


def place_kernel(at_ref, own_ref, got_ref, out_ref):
    out_ref[...] = jnp.zeros_like(out_ref)
    for i in range(GROUP):
        rows = slice(i * TOK, (i + 1) * TOK)
        total = own_ref[rows, :].astype(F32) + got_ref[rows, :].astype(F32)
        out_ref[pl.ds(pl.multiple_of(at_ref[i] * TOK, TOK), TOK), :] = total.astype(BF)


def place(at, own, got, chips):
    return pl.pallas_call(
        place_kernel,
        grid=(1,),
        in_specs=[pl.BlockSpec(memory_space=pltpu.SMEM), whole(own.shape), whole(got.shape)],
        out_specs=whole((chips * TOK, D)),
        out_shape=jax.ShapeDtypeStruct((chips * TOK, D), BF),
        compiler_params=params(16),
    )(at, own, got)


NEAR = ((0, 1, -1, 2), (0, 1, -1, -2))
FAR = ((-2, 3, -3, 4), (2, 3, -3, 4))


def along_z(i, way, n):
    return [(j, (j + 2 * way * NEAR[j % 2][i]) % n) for j in range(n)]


def along_x(d):
    return [(i, (i // SIDE) * SIDE + (i % SIDE + d) % SIDE) for i in range(SIDE * SIDE)]


def along_y(d):
    return [(i, i + SIDE * d) for i in range(SIDE * (SIDE - d))]


def local(
    query_raw,
    key_raw,
    values,
    out_gate,
    log_decay,
    beta_rate,
    head_gain,
    out_weight,
    residual,
    post_gain,
    router_weight,
    routes,
    placement,
    expert_in,
    expert_out,
):
    n_exp = lax.axis_size("exp")
    experts = router_weight.shape[1]
    at_exp = lax.axis_index("exp")
    at_x = (lax.axis_index("ctx") % SIDE).reshape(1)
    parity = (at_exp % 2).reshape(1)
    core_pairs = [(i, i ^ 1) for i in range(n_exp)]
    same_core = [list(range(0, n_exp, 2)), list(range(1, n_exp, 2))]

    weight_sib = lax.ppermute(out_weight, "exp", core_pairs)

    g, o, z = delta_local(query_raw, key_raw, values, log_decay, beta_rate)
    near = [lax.ppermute(z, "ctx", along_x(d)) for d in range(1, SIDE)]
    total, prefix = pl.pallas_call(
        fold_kernel,
        grid=(1,),
        out_shape=(jax.ShapeDtypeStruct(z.shape, BF), jax.ShapeDtypeStruct(z.shape, F32)),
        in_specs=[pl.BlockSpec(memory_space=pltpu.SMEM)] + [whole(z.shape)] * 4,
        out_specs=(whole(z.shape), whole(z.shape)),
        compiler_params=params(56),
    )(at_x, z, *near)
    far = [lax.ppermute(total, "ctx", along_y(d)) for d in range(1, SIDE)]
    core_out, mine, sib = core_local(parity, g, o, prefix, far, out_gate, head_gain.reshape(1, K))

    got = lax.ppermute(sib, "exp", core_pairs)
    terms = project(mine, got, out_weight, weight_sib)
    terms, routes = lax.optimization_barrier((terms, routes))
    attn = lax.psum_scatter(
        terms, "exp", scatter_dimension=0, tiled=True, axis_index_groups=same_core
    )
    routes_all = lax.all_gather(routes, "exp", tiled=True)
    rows = routes_all.shape[0]
    chips = n_exp // 2
    at_z = at_exp // 2
    at_core = at_exp % 2
    shift = jnp.where(
        at_core == 0,
        jnp.asarray(NEAR[0] + NEAR[1] + FAR[0] + FAR[1], jnp.int32),
        jnp.asarray(NEAR[1] + NEAR[0] + FAR[1] + FAR[0], jnp.int32),
    )
    flip = jnp.asarray(([0] * GROUP + [1] * GROUP) * 2, jnp.int32)
    order = 2 * ((at_z + shift) % chips) + (at_core + flip) % 2
    routes_rel = routes_all.reshape(n_exp, TOK, -1)[order].reshape(rows, -1)
    ids = jnp.arange(experts, dtype=jnp.int32)
    chosen = jnp.any(routes_rel[:, :, None] == ids[None, None, :], axis=1)
    wide = n_exp * GROUP * CAP
    lanes = jnp.arange(wide, dtype=jnp.int32)
    holder = (lanes // (GROUP * CAP)) * n_exp + at_exp
    spread = (placement[:, None] == holder[None, :]).astype(BF)
    named = jnp.dot(chosen.astype(BF), spread, preferred_element_type=F32)
    step = jnp.arange(TOK, dtype=jnp.int32)
    before = (step[:, None] > step[None, :]).astype(BF)
    rank = jnp.einsum(
        "ts,bsl->btl",
        before,
        named.astype(BF).reshape(rows // TOK, TOK, wide),
        preferred_element_type=F32,
    ).reshape(rows, wide)
    block = (jnp.arange(rows, dtype=jnp.int32) // TOK) % GROUP
    sel = (
        (named > 0.5)
        & (rank == (lanes % CAP).astype(F32)[None, :])
        & (block[:, None] == ((lanes // CAP) % GROUP)[None, :])
    )
    picks = sel.astype(BF)
    half_rows = rows // 2
    far_order = order[rows // TOK // 2 :]
    attn, picks, chosen, far_order = lax.optimization_barrier((attn, picks, chosen, far_order))
    mid, normed = norm_rows(residual, attn, post_gain.reshape(1, D))
    mid = mid.astype(F32)
    around = [lax.ppermute(normed, "exp", along_z(i, -1, n_exp)) for i in range(1, GROUP)]
    near_mine = [normed] + around
    near_sib = [lax.ppermute(a, "exp", core_pairs) for a in near_mine]
    normed_all = lax.all_gather(normed, "exp", tiled=True)

    def spread_out(rows):
        return lax.all_to_all(rows, "ctx", split_axis=0, concat_axis=0, tiled=True)

    def experts_on(rows):
        return expert(rows.reshape(-1, D), expert_in[0], expert_out[0]).reshape(rows.shape)

    near_rows = dispatch_near(picks[:half_rows], *near_mine, *near_sib)
    near_in = spread_out(near_rows)
    near_in, normed_far = lax.optimization_barrier((near_in, normed_all))
    far_rows = dispatch_far(far_order, picks[half_rows:], normed_far)
    far_in = spread_out(far_rows)
    near_out = experts_on(near_in)
    far_out = experts_on(far_in)

    logits = jnp.dot(normed_far, router_weight, preferred_element_type=F32)
    logits = logits.reshape(n_exp, TOK, experts)[order].reshape(rows, experts)
    raised = jnp.where(chosen, jnp.exp(logits), 0.0)
    gates = raised / jnp.sum(raised, axis=-1, keepdims=True)
    mine_gates = jnp.dot(gates, spread.astype(F32), precision=lax.Precision.HIGHEST)
    weights = jnp.where(sel, mine_gates, 0.0).astype(BF).reshape(4, rows // 4, wide)
    weights = lax.optimization_barrier([weights[i] for i in range(4)])

    far_back = spread_out(far_out)
    near_out, far_back = lax.optimization_barrier((near_out, far_back))

    far_got = lax.ppermute(combine(weights[3], far_back, 1), "exp", core_pairs)
    far_own = combine(weights[2], far_back, 0)
    far_shift = jnp.where(at_core == 0, *[jnp.asarray(a, jnp.int32) for a in FAR])
    far_placed = place((at_z + far_shift + chips) % chips, far_own, far_got, chips)
    near_out, far_placed = lax.optimization_barrier((near_out, far_placed))
    near_back = spread_out(near_out)
    far_sum = lax.psum_scatter(
        far_placed, "exp", scatter_dimension=0, tiled=True, axis_index_groups=same_core
    )

    near_got = lax.ppermute(combine(weights[1], near_back, 1), "exp", core_pairs)
    near_own = combine(weights[0], near_back, 0)
    near_sum = (near_own.astype(F32) + near_got.astype(F32)).reshape(GROUP, TOK, D)
    mixture = near_sum[0] + far_sum.astype(F32)
    for i in (3, 1, 2):
        sent = lax.ppermute(near_sum[i].astype(BF), "exp", along_z(i, 1, n_exp))
        mixture += sent.astype(F32)
    return (core_out, (mid + mixture).astype(BF))


def solution(mesh):
    placed = (
        P("ctx", "exp"),
        P("ctx", "exp"),
        P("ctx", "exp"),
        P("ctx", "exp"),
        P("exp", "ctx"),
        P("exp", "ctx"),
        P(),
        P("exp", None),
        P(("ctx", "exp"), None),
        P(),
        P(),
        P(("ctx", "exp"), None),
        P(),
        P(("ctx", "exp"), None, None),
        P(("ctx", "exp"), None, None),
    )
    return jax.shard_map(
        local,
        mesh=mesh,
        in_specs=placed,
        out_specs=(P("ctx", "exp"), P(("ctx", "exp"), None)),
        check_vma=False,
    )
```

```python
import math

import jax
import jax.numpy as jnp
from jax import lax
from jax.experimental import pallas as pl
from jax.experimental.pallas import tpu as pltpu
from jax.sharding import PartitionSpec as P

F32=jnp.float32; BF=jnp.bfloat16
EPS=1e-6
C=64
K=128
UNROLL = 16

def mm(a,b):
    return lax.dot_general(a,b,(((1,),(0,)),((),())),preferred_element_type=F32)

def split(a):
    hi=a.astype(BF)
    return hi,(a-hi.astype(F32)).astype(BF)

def mm3(a,b):
    ah,al=split(a); bh,bl=split(b)
    n=b.shape[1]
    if n==K:
        r=mm(jnp.concatenate([ah,al],1),jnp.concatenate([jnp.concatenate([bh,bl],1)]*2,0))
        return r[:,:n]+r[:,n:]
    return mm(jnp.concatenate([ah,al],1),jnp.concatenate([bh,bh],0))+mm(ah,bl)

def mm2(a,b):
    bh,bl=split(b)
    return mm(jnp.concatenate([a,a],1),jnp.concatenate([bh,bl],0))

def mm2l(a,b):
    ah,al=split(a)
    return mm(jnp.concatenate([ah,al],1),jnp.concatenate([b,b],0))

def mm1(a,b):
    return mm(a.astype(BF),b.astype(BF))

def delta_kernel(q_ref,k_ref,v_ref,row_ref,col_ref,go_g,go_o,z_out,wq_s,u_s,p_s,kw_s,dr_s,el_s):
    n=q_ref.shape[0]//C
    rows=lax.broadcasted_iota(jnp.int32,(2*C,2*C),0)
    cols=lax.broadcasted_iota(jnp.int32,(2*C,2*C),1)
    same=(rows//C)==(cols//C)
    strict=same&(rows>cols)
    within=same&(rows>=cols)
    lane=lax.broadcasted_iota(jnp.int32,(2*C,128),1)
    half=lax.broadcasted_iota(jnp.int32,(2*C,1),0)<C
    levels=[]
    b=1
    while b<C:
        levels.append(strict&((rows//(2*b))==(cols//(2*b)))&((rows//b)!=(cols//b)))
        b*=2
    def unit(m):
        return m*lax.rsqrt(jnp.sum(m*m,axis=-1,keepdims=True)+EPS)
    def prep(step,carry):
        amat=[];xs=[];rhs=[];kts=[];ids=[]
        allc=col_ref[...]
        for u in range(UNROLL):
            c=step*UNROLL+u
            ids.append(c)
            at=pl.ds(pl.multiple_of(c*C,C),C)
            kb=k_ref[at,:]
            qb=q_ref[at,:]
            k2=jnp.concatenate([kb,kb],0)
            q2=jnp.concatenate([qb,qb],0)
            kt=k2.T
            raw=mm(jnp.concatenate([k2,q2],0),kt)
            kf=k2.astype(F32)
            qf=q2.astype(F32)
            sk=lax.rsqrt(jnp.sum(kf*kf,axis=-1,keepdims=True)+EPS)
            sq=lax.rsqrt(jnp.sum(qf*qf,axis=-1,keepdims=True)+EPS)*(1.0/math.sqrt(K))
            sk_row=lax.rsqrt(jnp.sum(jnp.where(rows==cols,raw[:2*C],0.0),axis=0,keepdims=True)+EPS)
            g_row=row_ref[pl.ds(c,1),:]
            last_row=row_ref[pl.ds(n+c,1),:]
            b_row=row_ref[pl.ds(2*n+c,1),:]
            g_col=jnp.sum(jnp.where(lane==c,allc,0.0),axis=1,keepdims=True)
            b_col=jnp.sum(jnp.where(lane==n+c,allc,0.0),axis=1,keepdims=True)
            l_col=jnp.sum(jnp.where(lane==2*n+c,allc,0.0),axis=1,keepdims=True)
            fall=jnp.exp(jnp.where(within,g_col-g_row,0.0))*sk_row
            a=jnp.where(strict,fall*(b_col*sk)*raw[:2*C],0.0)
            p_s[c]=jnp.where(within,fall*sq*raw[2*C:],0.0).astype(BF)
            eg=jnp.exp(g_col)
            vb=v_ref[at,:]
            v2=jnp.concatenate([vb[:,:K],vb[:,K:]],0)
            rhs.append((b_row*jnp.exp(g_row)*sk_row,b_row,k2,v2))
            wq_s[c,1]=((eg*sq)*qf).astype(BF)
            kts.append((kt,sk*jnp.exp(l_col-g_col)))
            el_s[c]=jnp.exp(last_row)
            amat.append(a)
            xs.append(jnp.where(rows==cols,1.0,0.0)-jnp.where(levels[0],a,0.0))
        for lev in levels[1:]:
            mids=[mm3(jnp.where(lev,a,0.0),x) for a,x in zip(amat,xs)]
            xs=[x-mm3(x,m) for x,m in zip(xs,mids)]
        for c,x,(wr,br,k2,v2),(kt,kc) in zip(ids,xs,rhs,kts):
            w=mm2l(x*wr,k2)
            u=mm2l(x*br,v2)
            wq_s[c,0]=w.astype(BF)
            u_s[c]=u
            wu=jnp.concatenate([w,u],1)*kc
            both=jnp.concatenate([jnp.where(half,wu,0.0),jnp.where(half,0.0,wu)],1)
            td=mm2(kt,both)
            for h in range(2):
                kw_s[h,c]=td[:,h*2*K:h*2*K+K]
                dr_s[h,c]=td[:,h*2*K+K:(h+1)*2*K]
        return carry
    lax.fori_loop(0,n//UNROLL,prep,0)
    eye=jnp.where(lax.broadcasted_iota(jnp.int32,(K,K),0)==lax.broadcasted_iota(jnp.int32,(K,K),1),1.0,0.0)
    start=jnp.concatenate([eye,jnp.zeros((K,K),F32)],1)
    def chain(c,zs):
        new=[];fresh=[];outs=[]
        el=el_s[c]
        for h in range(2):
            z=zs[h]
            zb=z.astype(BF)
            e=jnp.sum(jnp.where(lax.broadcasted_iota(jnp.int32,(1,2*C),1)==h*C,el,0.0),axis=1,keepdims=True)
            t=e*z-mm3(kw_s[h,c],z)
            new.append(jnp.concatenate([t[:,:K],t[:,K:]+dr_s[h,c]],1))
            w=wq_s[c,0,h*C:(h+1)*C,:]
            q=wq_s[c,1,h*C:(h+1)*C,:]
            r=mm(jnp.concatenate([w,q],0),zb)
            f=-r[:C]
            uu=u_s[c,h*C:(h+1)*C,:]
            fresh.append(jnp.concatenate([f[:,:K],f[:,K:]+uu],1))
            outs.append(r[C:])
        out=jnp.concatenate(outs,0)+mm(p_s[c],jnp.concatenate(fresh,0).astype(BF))
        at=pl.ds(pl.multiple_of(c*C,C),C)
        for h in range(2):
            go_g[h,at,:]=out[h*C:(h+1)*C,:K].astype(BF)
            go_o[h,at,:]=out[h*C:(h+1)*C,K:]
        return tuple(new)
    zs=lax.fori_loop(0,n,chain,(start,start),unroll=8)
    for h in range(2):
        z_out[h]=zs[h].astype(BF)

def whole(shape):
    return pl.BlockSpec(tuple(shape),lambda *_: (0,)*len(shape))

def delta_local(q,k,v,ld,beta):
    t=q.shape[0]; n=t//C
    g=jnp.cumsum(ld.reshape(2,n,C),axis=-1)
    last=jnp.broadcast_to(g[:,:,-1:],g.shape)
    pack=lambda a: jnp.transpose(a,(1,0,2)).reshape(n,2*C)
    rate=pack(beta.reshape(2,n,C))
    row=jnp.concatenate([pack(g),pack(last),rate],0)
    col=jnp.concatenate([pack(g).T,rate.T,pack(last).T,jnp.zeros((2*C,128-3*n),F32)],1)
    shapes=[((2,t,K),BF),((2,t,K),F32),((2,K,2*K),BF)]
    return pl.pallas_call(
        delta_kernel,
        grid=(1,),
        out_shape=[jax.ShapeDtypeStruct(a,d) for a,d in shapes],
        in_specs=[whole(a.shape) for a in (q,k,v,row,col)],out_specs=[whole(a) for a,d in shapes],
        scratch_shapes=[pltpu.VMEM((n,2,2*C,K),BF),pltpu.VMEM((n,2*C,K),F32),pltpu.VMEM((n,2*C,2*C),BF),
            pltpu.VMEM((2,n,K,K),F32),pltpu.VMEM((2,n,K,K),F32),pltpu.VMEM((n,1,2*C),F32)],
        compiler_params=pltpu.CompilerParams(vmem_limit_bytes=56*2**20),
    )(q,k,v,row,col)

CAP = 4
GROUP = 4
TOK = 64
SIDE = 4
D = 2048


def params(mib):
    return pltpu.CompilerParams(vmem_limit_bytes=mib * 2**20)


def fold_kernel(x_ref, own, a1, a2, a3, total_ref, prefix_ref):
    x = x_ref[0]
    eye = jnp.where(
        lax.broadcasted_iota(jnp.int32, (K, K), 0) == lax.broadcasted_iota(jnp.int32, (K, K), 1),
        1.0,
        0.0,
    )
    for h in range(2):
        near = [own[h].astype(F32), a1[h].astype(F32), a2[h].astype(F32), a3[h].astype(F32)]
        z = jnp.concatenate([eye, jnp.zeros((K, K), F32)], 1)
        prefix = z
        for j in range(SIDE):
            item = near[0]
            for d in range(1, SIDE):
                item = jnp.where((x - j) % SIDE == d, near[d], item)
            if j == 0:
                z = item
            else:
                zh, zl = split(z)
                m = item[:, :K].astype(BF)
                t = mm(m, zh) + mm(m, zl)
                z = jnp.concatenate([t[:, :K], t[:, K:] + item[:, K:]], 1)
            if j < SIDE - 1:
                prefix = jnp.where(x == j + 1, z, prefix)
        total_ref[h] = z.astype(BF)
        prefix_ref[h] = prefix


def core_kernel(
    par_ref, g_ref, o_ref, prefix, b1, b2, b3, gate_ref, gain_ref, core_ref, mine, sib, state
):
    gain = gain_ref[...]
    even = par_ref[0] == 0

    @pl.when(pl.program_id(0) == 0)
    def _():
        for h in range(2):
            e = b3[h][:, K:].astype(F32)
            for b in (b2, b1):
                eh, el = split(e)
                m = b[h][:, :K]
                e = mm(m, eh) + mm(m, el) + b[h][:, K:].astype(F32)
            e = mm3(prefix[h][:, :K], e) + prefix[h][:, K:]
            eh, el = split(e)
            state[h] = jnp.concatenate([eh, el], 1)

    step = 2 * TOK
    for i in range(g_ref.shape[1] // step):
        at = slice(i * step, (i + 1) * step)
        outs = []
        for h in range(2):
            both = mm(g_ref[h, at, :], state[h])
            core = o_ref[h, at, :] + both[:, :K] + both[:, K:]
            gate = gate_ref[at, h * K : (h + 1) * K].astype(F32)
            scaled = core * lax.rsqrt(jnp.mean(core * core, axis=-1, keepdims=True) + EPS)
            outs.append((scaled * gain * (gate / (1.0 + jnp.exp(-gate)))).astype(BF))
        out = jnp.concatenate(outs, 1)
        core_ref[at, :] = out
        to = slice(i * TOK, (i + 1) * TOK)
        mine[to, :] = jnp.where(even, out[:TOK], out[TOK:])
        sib[to, :] = jnp.where(even, out[TOK:], out[:TOK])


def core_local(parity, g, o, prefix, far, gate, gain):
    rows, wide = gate.shape
    part = 512
    half = jax.ShapeDtypeStruct((rows // 2, wide), BF)
    heads = pl.BlockSpec((2, part, K), lambda i: (0, i, 0))
    half_spec = pl.BlockSpec((part // 2, wide), lambda i: (i, 0))
    full_spec = pl.BlockSpec((part, wide), lambda i: (i, 0))
    return pl.pallas_call(
        core_kernel,
        grid=(rows // part,),
        out_shape=(jax.ShapeDtypeStruct(gate.shape, BF), half, half),
        in_specs=[pl.BlockSpec(memory_space=pltpu.SMEM), heads, heads]
        + [whole(prefix.shape)] * 4
        + [full_spec, whole(gain.shape)],
        out_specs=(full_spec, half_spec, half_spec),
        scratch_shapes=[pltpu.VMEM((2, K, 2 * K), BF)],
        compiler_params=params(56),
    )(parity, g, o, prefix, *far, gate, gain)


def project_kernel(a_ref, b_ref, wa_ref, wb_ref, out_ref):
    out_ref[...] = (mm(a_ref[...], wa_ref[...]) + mm(b_ref[...], wb_ref[...])).astype(BF)


def project(a, b, wa, wb):
    rows, depth = a.shape
    wide = 512
    return pl.pallas_call(
        project_kernel,
        grid=(D // wide,),
        out_shape=jax.ShapeDtypeStruct((rows, D), BF),
        in_specs=[
            pl.BlockSpec((rows, depth), lambda i: (0, 0)),
            pl.BlockSpec((rows, depth), lambda i: (0, 0)),
            pl.BlockSpec((depth, wide), lambda i: (0, i)),
            pl.BlockSpec((depth, wide), lambda i: (0, i)),
        ],
        out_specs=pl.BlockSpec((rows, wide), lambda i: (0, i)),
        compiler_params=params(16),
    )(a, b, wa, wb)


def norm_kernel(res_ref, attn_ref, gain_ref, mid_ref, normed_ref):
    mid = (res_ref[...].astype(F32) + attn_ref[...].astype(F32)).astype(BF)
    mid_ref[...] = mid
    mid = mid.astype(F32)
    scale = lax.rsqrt(jnp.mean(mid * mid, axis=-1, keepdims=True) + EPS)
    normed_ref[...] = (mid * scale * gain_ref[...]).astype(BF)


def norm_rows(residual, attn, gain):
    spec = whole(residual.shape)
    shape = jax.ShapeDtypeStruct(residual.shape, BF)
    return pl.pallas_call(
        norm_kernel,
        grid=(1,),
        out_shape=(shape, shape),
        in_specs=[spec, spec, whole(gain.shape)],
        out_specs=(spec, spec),
        compiler_params=params(16),
    )(residual, attn, gain)


def pick(sel, rows):
    out = lax.dot_general(sel, rows, (((0,), (0,)), ((), ())), preferred_element_type=F32)
    return out.astype(BF).reshape(sel.shape[1] // (GROUP * CAP), GROUP * CAP, D)


def near_kernel(sel_ref, *refs):
    *parts, out_ref = refs
    mine = jnp.concatenate([a[...] for a in parts[:GROUP]], 0)
    sib = jnp.concatenate([a[...] for a in parts[GROUP:]], 0)
    out_ref[:, : GROUP * CAP, :] = pick(sel_ref[: GROUP * TOK], mine)
    out_ref[:, GROUP * CAP :, :] = pick(sel_ref[GROUP * TOK :], sib)


def dispatch_near(sel, *parts):
    return pl.pallas_call(
        near_kernel,
        grid=(1,),
        out_shape=jax.ShapeDtypeStruct((16, 2 * GROUP * CAP, D), BF),
        in_specs=[whole(sel.shape)] + [whole(a.shape) for a in parts],
        out_specs=whole((16, 2 * GROUP * CAP, D)),
        compiler_params=params(16),
    )(sel, *parts)


def far_kernel(order_ref, sel_ref, r0, r1, r2, r3, out_ref):
    rows = jnp.concatenate([r0[...], r1[...], r2[...], r3[...]], 0)
    out_ref[...] = pick(sel_ref[...], rows)


def dispatch_far(order, sel, rows):
    part = GROUP * TOK

    def block(j):
        return pl.BlockSpec((TOK, D), lambda g, order: (order[GROUP * g + j], 0))

    return pl.pallas_call(
        far_kernel,
        grid_spec=pltpu.PrefetchScalarGridSpec(
            num_scalar_prefetch=1,
            grid=(2,),
            in_specs=[pl.BlockSpec((part, sel.shape[1]), lambda g, order: (g, 0))]
            + [block(j) for j in range(GROUP)],
            out_specs=pl.BlockSpec((16, GROUP * CAP, D), lambda g, order: (0, g, 0)),
        ),
        out_shape=jax.ShapeDtypeStruct((16, 2 * GROUP * CAP, D), BF),
        compiler_params=params(16),
    )(order, sel, rows, rows, rows, rows)


def expert_kernel(x_ref, gate_ref, up_ref, down_ref, out_ref, total):
    x = x_ref[...]
    gate = mm(x, gate_ref[...])
    act = (gate / (1.0 + jnp.exp(-gate)) * mm(x, up_ref[...])).astype(BF)
    term = mm(act, down_ref[...])
    step = pl.program_id(0)

    @pl.when(step == 0)
    def _():
        total[...] = term

    @pl.when(step > 0)
    def _():
        out_ref[...] = (total[...] + term).astype(BF)


def expert(x, gate_up, down):
    part = down.shape[0] // 2
    return pl.pallas_call(
        expert_kernel,
        grid=(2,),
        out_shape=jax.ShapeDtypeStruct(x.shape, BF),
        in_specs=[
            whole(x.shape),
            pl.BlockSpec((D, part), lambda i: (0, i)),
            pl.BlockSpec((D, part), lambda i: (0, 2 + i)),
            pl.BlockSpec((part, D), lambda i: (i, 0)),
        ],
        out_specs=whole(x.shape),
        scratch_shapes=[pltpu.VMEM(x.shape, F32)],
        cost_estimate=pl.CostEstimate(
            flops=6 * x.shape[0] * D * down.shape[0], bytes_accessed=10 * 2**20, transcendentals=0
        ),
        compiler_params=params(32),
    )(x, gate_up, gate_up, down)


def combine_kernel(w_ref, y_ref, out_ref):
    rows = y_ref[...].reshape(w_ref.shape[1], D)
    out_ref[...] = mm(w_ref[...], rows).astype(BF)


def combine(weights, y, half):
    part = GROUP * TOK
    return pl.pallas_call(
        combine_kernel,
        grid=(1,),
        out_shape=jax.ShapeDtypeStruct((part, D), BF),
        in_specs=[
            whole(weights.shape),
            pl.BlockSpec((y.shape[0], GROUP * CAP, D), lambda i: (0, half, 0)),
        ],
        out_specs=whole((part, D)),
        compiler_params=params(16),
    )(weights, y)


def blocks_kernel(w_ref, y_ref, *out_refs):
    rows = y_ref[...].reshape(w_ref.shape[1], D)
    out = mm(w_ref[...], rows).astype(BF)
    for i, out_ref in enumerate(out_refs):
        out_ref[...] = out[i * TOK : (i + 1) * TOK]


def combine_blocks(weights, y, half):
    block = jax.ShapeDtypeStruct((TOK, D), BF)
    return pl.pallas_call(
        blocks_kernel,
        grid=(1,),
        out_shape=[block] * GROUP,
        in_specs=[
            whole(weights.shape),
            pl.BlockSpec((y.shape[0], GROUP * CAP, D), lambda i: (0, half, 0)),
        ],
        out_specs=[whole(block.shape)] * GROUP,
        compiler_params=params(16),
    )(weights, y)


def place_kernel(at_ref, own_ref, got_ref, out_ref):
    out_ref[...] = jnp.zeros_like(out_ref)
    for i in range(GROUP):
        rows = slice(i * TOK, (i + 1) * TOK)
        total = own_ref[rows, :].astype(F32) + got_ref[rows, :].astype(F32)
        out_ref[pl.ds(pl.multiple_of(at_ref[i] * TOK, TOK), TOK), :] = total.astype(BF)


def place(at, own, got, chips):
    return pl.pallas_call(
        place_kernel,
        grid=(1,),
        in_specs=[pl.BlockSpec(memory_space=pltpu.SMEM), whole(own.shape), whole(got.shape)],
        out_specs=whole((chips * TOK, D)),
        out_shape=jax.ShapeDtypeStruct((chips * TOK, D), BF),
        compiler_params=params(16),
    )(at, own, got)


NEAR = ((0, 1, -1, 2), (0, 1, -1, -2))
FAR = ((-2, 3, -3, 4), (2, 3, -3, 4))


def along_z(i, way, n):
    return [(j, (j + 2 * way * NEAR[j % 2][i]) % n) for j in range(n)]


def along_x(d):
    return [(i, (i // SIDE) * SIDE + (i % SIDE + d) % SIDE) for i in range(SIDE * SIDE)]


def along_y(d):
    return [(i, i + SIDE * d) for i in range(SIDE * (SIDE - d))]


def local(
    query_raw,
    key_raw,
    values,
    out_gate,
    log_decay,
    beta_rate,
    head_gain,
    out_weight,
    residual,
    post_gain,
    router_weight,
    routes,
    placement,
    expert_in,
    expert_out,
):
    n_exp = lax.axis_size("exp")
    experts = router_weight.shape[1]
    at_exp = lax.axis_index("exp")
    at_x = (lax.axis_index("ctx") % SIDE).reshape(1)
    parity = (at_exp % 2).reshape(1)
    core_pairs = [(i, i ^ 1) for i in range(n_exp)]
    same_core = [list(range(0, n_exp, 2)), list(range(1, n_exp, 2))]

    weight_sib = lax.ppermute(out_weight, "exp", core_pairs)

    g, o, z = delta_local(query_raw, key_raw, values, log_decay, beta_rate)
    near = [lax.ppermute(z, "ctx", along_x(d)) for d in range(1, SIDE)]
    total, prefix = pl.pallas_call(
        fold_kernel,
        grid=(1,),
        out_shape=(jax.ShapeDtypeStruct(z.shape, BF), jax.ShapeDtypeStruct(z.shape, F32)),
        in_specs=[pl.BlockSpec(memory_space=pltpu.SMEM)] + [whole(z.shape)] * 4,
        out_specs=(whole(z.shape), whole(z.shape)),
        compiler_params=params(56),
    )(at_x, z, *near)
    far = [lax.ppermute(total, "ctx", along_y(d)) for d in range(1, SIDE)]
    core_out, mine, sib = core_local(parity, g, o, prefix, far, out_gate, head_gain.reshape(1, K))

    got = lax.ppermute(sib, "exp", core_pairs)
    terms = project(mine, got, out_weight, weight_sib)
    terms, routes = lax.optimization_barrier((terms, routes))
    attn = lax.psum_scatter(
        terms, "exp", scatter_dimension=0, tiled=True, axis_index_groups=same_core
    )
    routes_all = lax.all_gather(routes, "exp", tiled=True)
    rows = routes_all.shape[0]
    chips = n_exp // 2
    at_z = at_exp // 2
    at_core = at_exp % 2
    shift = jnp.where(
        at_core == 0,
        jnp.asarray(NEAR[0] + NEAR[1] + FAR[0] + FAR[1], jnp.int32),
        jnp.asarray(NEAR[1] + NEAR[0] + FAR[1] + FAR[0], jnp.int32),
    )
    flip = jnp.asarray(([0] * GROUP + [1] * GROUP) * 2, jnp.int32)
    order = 2 * ((at_z + shift) % chips) + (at_core + flip) % 2
    routes_rel = routes_all.reshape(n_exp, TOK, -1)[order].reshape(rows, -1)
    ids = jnp.arange(experts, dtype=jnp.int32)
    chosen = jnp.any(routes_rel[:, :, None] == ids[None, None, :], axis=1)
    wide = n_exp * GROUP * CAP
    lanes = jnp.arange(wide, dtype=jnp.int32)
    holder = (lanes // (GROUP * CAP)) * n_exp + at_exp
    spread = (placement[:, None] == holder[None, :]).astype(BF)
    named = jnp.dot(chosen.astype(BF), spread, preferred_element_type=F32)
    step = jnp.arange(TOK, dtype=jnp.int32)
    before = (step[:, None] > step[None, :]).astype(BF)
    rank = jnp.einsum(
        "ts,bsl->btl",
        before,
        named.astype(BF).reshape(rows // TOK, TOK, wide),
        preferred_element_type=F32,
    ).reshape(rows, wide)
    block = (jnp.arange(rows, dtype=jnp.int32) // TOK) % GROUP
    sel = (
        (named > 0.5)
        & (rank == (lanes % CAP).astype(F32)[None, :])
        & (block[:, None] == ((lanes // CAP) % GROUP)[None, :])
    )
    picks = sel.astype(BF)
    half_rows = rows // 2
    far_order = order[rows // TOK // 2 :]
    attn, picks, chosen, far_order = lax.optimization_barrier((attn, picks, chosen, far_order))
    mid, normed = norm_rows(residual, attn, post_gain.reshape(1, D))
    mid = mid.astype(F32)
    around = [lax.ppermute(normed, "exp", along_z(i, -1, n_exp)) for i in range(1, GROUP)]
    near_mine = [normed] + around
    near_sib = [lax.ppermute(a, "exp", core_pairs) for a in near_mine]
    normed_all = lax.all_gather(normed, "exp", tiled=True)

    def spread_out(rows):
        return lax.all_to_all(rows, "ctx", split_axis=0, concat_axis=0, tiled=True)

    def experts_on(rows):
        return expert(rows.reshape(-1, D), expert_in[0], expert_out[0]).reshape(rows.shape)

    near_rows = dispatch_near(picks[:half_rows], *near_mine, *near_sib)
    near_in = spread_out(near_rows)
    near_in, normed_far = lax.optimization_barrier((near_in, normed_all))
    far_rows = dispatch_far(far_order, picks[half_rows:], normed_far)
    far_in = spread_out(far_rows)
    near_out = experts_on(near_in)
    far_out = experts_on(far_in)

    logits = jnp.dot(normed_far, router_weight, preferred_element_type=F32)
    logits = logits.reshape(n_exp, TOK, experts)[order].reshape(rows, experts)
    raised = jnp.where(chosen, jnp.exp(logits), 0.0)
    gates = raised / jnp.sum(raised, axis=-1, keepdims=True)
    mine_gates = jnp.dot(gates, spread.astype(F32), precision=lax.Precision.HIGHEST)
    weights = jnp.where(sel, mine_gates, 0.0).astype(BF).reshape(4, rows // 4, wide)
    weights = lax.optimization_barrier([weights[i] for i in range(4)])

    far_back = spread_out(far_out)
    near_out, far_back = lax.optimization_barrier((near_out, far_back))

    far_got = lax.ppermute(combine(weights[3], far_back, 1), "exp", core_pairs)
    far_own = combine(weights[2], far_back, 0)
    far_shift = jnp.where(at_core == 0, *[jnp.asarray(a, jnp.int32) for a in FAR])
    far_placed = place((at_z + far_shift + chips) % chips, far_own, far_got, chips)
    near_out, far_placed = lax.optimization_barrier((near_out, far_placed))
    near_back = spread_out(near_out)
    far_sum = lax.psum_scatter(
        far_placed, "exp", scatter_dimension=0, tiled=True, axis_index_groups=same_core
    )

    near_sent = combine_blocks(weights[1], near_back, 1)
    near_got = {i: lax.ppermute(near_sent[i], "exp", core_pairs) for i in (3, 1, 2, 0)}
    near_own = combine_blocks(weights[0], near_back, 0)
    near_sum = [near_own[i].astype(F32) + near_got[i].astype(F32) for i in range(GROUP)]
    mixture = near_sum[0] + far_sum.astype(F32)
    for i in (3, 1, 2):
        sent = lax.ppermute(near_sum[i].astype(BF), "exp", along_z(i, 1, n_exp))
        mixture += sent.astype(F32)
    return (core_out, (mid + mixture).astype(BF))


def solution(mesh):
    placed = (
        P("ctx", "exp"),
        P("ctx", "exp"),
        P("ctx", "exp"),
        P("ctx", "exp"),
        P("exp", "ctx"),
        P("exp", "ctx"),
        P(),
        P("exp", None),
        P(("ctx", "exp"), None),
        P(),
        P(),
        P(("ctx", "exp"), None),
        P(),
        P(("ctx", "exp"), None, None),
        P(("ctx", "exp"), None, None),
    )
    return jax.shard_map(
        local,
        mesh=mesh,
        in_specs=placed,
        out_specs=(P("ctx", "exp"), P(("ctx", "exp"), None)),
        check_vma=False,
    )
```
